512 devices in a mesh: wave: 128 (over z, y, core), lev: 4 (over x).
Axes of the slice: x: 4, y: 4, z: 16, core: 2. Of those that a mesh axis runs over, the one named last changes fastest.
Arguments:
- coeffs: bfloat16 [768, 2, 4, 16, 768], P('wave', None, None, 'lev'), may hold values from -6 to 6
- legendre: bfloat16 [768, 768, 384], P('wave'), may hold values from -6 to 6
- slot_wave: int32 [768], replicated, may hold values from 0 to 767, as said below
- lon_points: int32 [768], replicated, may hold values from 20 to 3088, as said below
- quad_weights: float32 [768], replicated, may hold values from 0.5 to 1.5
Outputs:
- spectral_out: bfloat16 [768, 2, 4, 16, 768], P('wave', None, None, 'lev')
The draws below stay inside these ranges and needn't reach their ends.
Inputs may be any that keep to these rules, and one draw needn't show every extreme that they name: `slot_wave`: a permutation of the wavenumbers in which slots 2q and 2q+1 hold wavenumbers m and 767-m, so the 6 slots of one device are whole pairs. `lon_points`: every value is 4 i + 16 for a whole number i; values rise from latitude 0 to latitude 384 - 1, and lon_points[767-j] equals lon_points[j].
All inputs are finite; a program needn't handle non-finite values.
Results may differ from the reference program's by a relative error of at most 0.0075.
Values may be sent and summed in bfloat16 or wider, within the bound.
A program may use at most 64 MiB of HBM per device.

```python
import functools
import math
import jax
import jax.numpy as jnp
from jax import lax

WAVES = 768
FIELDS = 4
NLEV = 16
NLAT = 768
LATH = 384
LONPAD = 3584


def draw_slot_wave(key, part):
    key = jax.random.fold_in(key, 11)
    partners = jax.random.permutation(key, WAVES // 2).astype(jnp.int32)
    return jnp.stack([partners, WAVES - 1 - partners], axis=1).reshape(WAVES).astype(jnp.int32)


def draw_lon_points(key, part):
    key = jax.random.fold_in(key, 23)
    stride = WAVES // LATH
    offsets = jax.random.randint(key, (LATH,), 1, stride + 1).astype(jnp.int32)
    latitude = jnp.arange(LATH, dtype=jnp.int32)
    row_index = stride * latitude + offsets
    row_index = jnp.where(latitude == 0, 1, row_index)
    row_index = jnp.where(latitude == LATH - 1, WAVES, row_index)
    north_points = 4 * row_index + 16
    return jnp.concatenate([north_points, north_points[::-1]]).astype(jnp.int32)


def steps_of(rng, shape, split, low, high):
    loudness, own = 1.0, jax.random.fold_in(rng, 6)
    for dim, shards_of in split:
        draws = jnp.exp(jax.random.uniform(jax.random.fold_in(own, dim), (shards_of,), jnp.float32, low / len(split), high / len(split)))
        loudness = loudness * jnp.repeat(draws, shape[dim] // shards_of).reshape([-1 if axis == dim else 1 for axis in range(len(shape))])
    return loudness


def centred(stream_key, shape, width, most, split=(), kind=jnp.bfloat16):
    values = jax.random.normal(stream_key, shape, jnp.float32) * width
    if len(split) > 0:
        values = steps_of(stream_key, shape, split, -0.22, 0.18) * values
    return jnp.clip(values, min=-most, max=most).astype(kind)


def setup_inputs(seed: int = 0) -> dict:
    seeds = jax.random.split(jax.random.key(seed), 6)
    coeffs = centred(seeds[0], (WAVES, 2, FIELDS, NLEV, WAVES), 1.0, 6.0, ((0, 128), (3, 4)))
    legendre = centred(seeds[1], (WAVES, WAVES, LATH), 1.0, 6.0, ((0, 128),))
    slot_wave = draw_slot_wave(jax.random.fold_in(seeds[5], 71), 0)
    lon_points = draw_lon_points(jax.random.fold_in(seeds[5], 71), 0)
    quad_weights = jnp.clip(jax.random.uniform(seeds[4], (NLAT,), jnp.float32, 0.5, 1.5), 0.5, 1.5)
    return dict(coeffs=coeffs, legendre=legendre, slot_wave=slot_wave, lon_points=lon_points, quad_weights=quad_weights)


TWO_PI = 2.0 * math.pi
degree_block = 64
highest = lax.Precision.HIGHEST

def legendre_masks(wave_numbers):
    degree = jnp.arange(WAVES, dtype=jnp.int32)
    keep_mask = (degree[None, :] >= wave_numbers[:, None]).astype(jnp.float32)
    parity = jnp.where((degree[None, :] + wave_numbers[:, None]) % 2 == 0, 1.0, -1.0).astype(jnp.float32)
    return (keep_mask, parity)

def inverse_group(operands):
    spec_group, table_group, wave_numbers = operands
    keep_mask, parity = legendre_masks(wave_numbers)
    masked = spec_group.astype(jnp.float32) * keep_mask[:, None, :]
    table_f32 = table_group.astype(jnp.float32)
    north_part = jnp.einsum('bcn,bnj->bcj', masked, table_f32)
    south_part = jnp.einsum('bcn,bnj->bcj', masked * parity[:, None, :], table_f32)
    return jnp.concatenate([north_part, south_part[:, :, ::-1]], axis=2) / math.sqrt(WAVES)

def latitude_step(slot_wave, operands):
    column, points, weight = operands
    half_count = FIELDS * NLEV
    top_wave = jnp.minimum(WAVES - 1, (points - 1) // 2)
    keep_wave = (slot_wave <= top_wave).astype(jnp.float32)
    factor = jnp.where(slot_wave == 0, 1.0, 2.0).astype(jnp.float32) * keep_wave / math.sqrt(WAVES)
    longitude = jnp.arange(LONPAD, dtype=jnp.int32)
    phases = slot_wave[:, None] * longitude[None, :] % points
    angles = phases.astype(jnp.float32) * (TWO_PI / points.astype(jnp.float32))
    cosine_table = jnp.cos(angles)
    sine_table = jnp.sin(angles)
    inside = (longitude < points).astype(jnp.float32)
    real_part = column[:, :half_count] * factor[:, None]
    imag_part = column[:, half_count:] * factor[:, None]
    grid_field = jnp.dot(real_part.T, cosine_table, precision=highest) - jnp.dot(imag_part.T, sine_table, precision=highest)
    grid_field = (grid_field * inside[None, :]).reshape(FIELDS, NLEV, LONPAD)
    level_scale = 1.0 / math.sqrt(NLEV)
    mass_sum = jnp.cumsum(grid_field[1], axis=0) * level_scale
    geopot = jnp.cumsum(grid_field[2], axis=0) * level_scale
    forcing = jnp.stack([grid_field[0] * grid_field[1], geopot, grid_field[2] * mass_sum, grid_field[3] + mass_sum])
    forcing = forcing.reshape(half_count, LONPAD)
    out_scale = keep_wave * math.sqrt(WAVES) / points.astype(jnp.float32)
    real_out = jnp.dot(cosine_table, forcing.T, precision=highest) * out_scale[:, None]
    imag_out = -jnp.dot(sine_table, forcing.T, precision=highest) * out_scale[:, None]
    return (weight * jnp.concatenate([real_out, imag_out], axis=1)).astype(jnp.bfloat16)

def direct_group(operands):
    grid_group, table_group, wave_numbers = operands
    keep_mask, parity = legendre_masks(wave_numbers)
    table_f32 = table_group.astype(jnp.float32)
    weighted = grid_group.astype(jnp.float32)
    north_part = jnp.einsum('bnj,bcj->bcn', table_f32, weighted[:, :, :LATH])
    south_part = jnp.einsum('bnj,bcj->bcn', table_f32, weighted[:, :, ::-1][:, :, :LATH])
    total = (north_part + parity[:, None, :] * south_part) * keep_mask[:, None, :] / math.sqrt(NLAT)
    return total.astype(jnp.bfloat16)

def reference(coeffs, legendre, slot_wave, lon_points, quad_weights):
    channels = 2 * FIELDS * NLEV
    group_count = WAVES // degree_block
    spectral = coeffs.reshape(group_count, degree_block, channels, WAVES)
    tables = legendre.reshape(group_count, degree_block, WAVES, LATH)
    wave_groups = slot_wave.reshape(group_count, degree_block)
    fourier = lax.map(inverse_group, (spectral, tables, wave_groups))
    fourier = fourier.reshape(WAVES, channels, NLAT).transpose(2, 0, 1)
    weighted = lax.map(functools.partial(latitude_step, slot_wave), (fourier, lon_points, quad_weights))
    weighted = weighted.transpose(1, 2, 0).reshape(group_count, degree_block, channels, NLAT)
    result = lax.map(direct_group, (weighted, tables, wave_groups))
    return result.reshape(WAVES, 2, FIELDS, NLEV, WAVES)
```

```python
import math

import numpy as np
import jax
import jax.numpy as jnp
from jax import lax
from jax.experimental import pallas as pl
from jax.experimental.pallas import tpu as pltpu
from jax.sharding import PartitionSpec as P

MESH = pl.DeviceIdType.MESH
f32 = jnp.float32
bf16 = jnp.bfloat16
SLOTS = 6
DEGREES = 768
HALF = 384
WAVE = 128
LEV = 4
LATS = 3
LANES = 128
WIDTH = 512
ROOT = 1.0 / math.sqrt(768.0)


def turn_polynomials(terms):
    x = np.cos(np.linspace(0.0, np.pi, 4001)) * 0.5
    y = x * x
    powers = np.stack([y**i for i in range(terms)], axis=1)
    cosine = np.linalg.lstsq(powers, np.cos(2 * np.pi * x), rcond=None)[0]
    sine = np.linalg.lstsq(powers * x[:, None], np.sin(2 * np.pi * x), rcond=None)[0]
    return [float(np.float32(c)) for c in cosine], [float(np.float32(c)) for c in sine]


COSINE, SINE = turn_polynomials(6)


def horner(coefficients, y):
    total = coefficients[-1]
    for c in coefficients[-2::-1]:
        total = total * y + c
    return total


def kernel(
    lon_s, slot_s, quad_s, waves_ref, lat_ref, coeffs_ref, legendre_ref, out_ref,
    sums, lev_send, lev_recv, lower, stage, four, column, tables, planes, wide,
    send_one, recv_one, send_two, recv_two, pairs, left, sumpq, leftback, planes_two, weighted,
    lev_ssem, lev_rsem, ssem_one, rsem_one, ssem_two, rsem_two,
):
    me = lax.axis_index("wave")
    lev = lax.axis_index("lev")
    barrier = pltpu.get_barrier_semaphore()

    def greet(i, carry):
        pl.semaphore_signal(barrier, inc=1, device_id=(lax.rem(me + i, WAVE), lev), device_id_type=MESH)
        return carry

    lax.fori_loop(1, WAVE, greet, 0)
    for i in range(1, LEV):
        pl.semaphore_signal(barrier, inc=1, device_id=(me, lax.rem(lev + i, LEV)), device_id_type=MESH)

    sums[24:32, :] = jnp.zeros((8, DEGREES), f32)
    for s in range(SLOTS):
        for r in range(2):
            for f in (1, 2):
                row = s * 4 + r * 2 + f - 1
                sums[row : row + 1, :] = jnp.sum(coeffs_ref[s, r, f].astype(f32), axis=0, keepdims=True)
    lev_send[...] = sums[...].astype(bf16)
    lev_recv[lev] = jnp.zeros((32, DEGREES), bf16)
    pl.semaphore_wait(barrier, WAVE - 1 + LEV - 1)
    for i in range(1, LEV):
        pltpu.make_async_remote_copy(
            src_ref=lev_send, dst_ref=lev_recv.at[lev], send_sem=lev_ssem, recv_sem=lev_rsem,
            device_id=(me, lax.rem(lev + i, LEV)), device_id_type=MESH,
        ).start()

    for q in range(3):
        first = waves_ref[2 * q : 2 * q + 1, :]
        second = waves_ref[2 * q + 1 : 2 * q + 2, :]
        even_first = (first & 1) == 0
        even = jnp.where(even_first, first, second)
        odd = jnp.where(even_first, second, first)
        column[q] = jnp.broadcast_to(even.astype(f32), (LANES, LANES)).T
        column[3 + q] = jnp.broadcast_to(odd.astype(f32), (LANES, LANES)).T

    def table_block(step, carry):
        t = step // 6
        c = lax.rem(step, 6)
        parity = c // 3
        q = lax.rem(c, 3)
        points = lon_s[me + LANES * t]
        per_point = 1.0 / jnp.full((1, LANES), points, jnp.int32).astype(f32)
        wave = column[c]
        lane = lax.broadcasted_iota(jnp.int32, (1, LANES), 1).astype(f32)
        for block in range(WIDTH // LANES):
            turn = wave * (lane + float(block * LANES)) * per_point
            x = turn - jnp.floor(turn + 0.5)
            y = x * x
            rows = pl.ds(pl.multiple_of(q * LANES, LANES), LANES)
            columns = pl.ds(block * LANES, LANES)
            tables[t, 2 * parity, rows, columns] = horner(COSINE, y).astype(bf16)
            tables[t, 2 * parity + 1, rows, columns] = (horner(SINE, y) * x).astype(bf16)
        return carry

    lax.fori_loop(0, LATS * 6, table_block, 0)

    everyone = pltpu.make_async_copy(lev_recv.at[pl.ds(0, LEV - 1)], lev_recv.at[pl.ds(0, LEV - 1)], lev_rsem)
    everyone.wait()
    pltpu.make_async_copy(lev_recv.at[pl.ds(0, LEV - 1)], lev_recv.at[pl.ds(0, LEV - 1)], lev_ssem).wait()
    total = jnp.zeros((32, DEGREES), f32)
    for k in range(LEV):
        total = total + jnp.where(k < lev, lev_recv[k].astype(f32), 0.0)
    sums[...] = total
    for s in range(SLOTS):
        lower[s, 0:4, :] = sums[s * 4 : s * 4 + 4, :]

    degree = lax.broadcasted_iota(jnp.int32, (1, DEGREES), 1)
    place = (0, 4, 2, 6)
    for b in range(DEGREES // LANES):
        stage[b, 72:80, :] = jnp.zeros((8, LANES), f32)

    def put_rows(start, stride, value):
        for b in range(DEGREES // LANES):
            stage[b, pl.ds(start, 4, stride=stride), :] = value[:, b * LANES : (b + 1) * LANES]

    def forward(s, carry):
        m = slot_s[me * SLOTS + s]
        keep = (degree >= m).astype(f32)
        flipped = keep * (1.0 - 2.0 * ((degree + m) & 1).astype(f32))
        for r in range(2):
            for f in range(4):
                value = coeffs_ref[s, r, f].astype(f32)
                put_rows(r * 32 + place[f], 8, value * keep)
                put_rows(r * 32 + place[f] + 1, 8, value * flipped)
        extra = lower[s, 0:4, :]
        put_rows(64, 2, extra * keep)
        put_rows(65, 2, extra * flipped)
        operand = jnp.concatenate([stage[b] for b in range(DEGREES // LANES)], axis=1).astype(bf16)
        product = jnp.dot(operand, legendre_ref[s], preferred_element_type=f32) * ROOT
        for t in range(LATS):
            four[s, t] = product[:, t * LANES : (t + 1) * LANES]
        return carry

    lax.fori_loop(0, SLOTS, forward, 0)

    def spread(step, carry):
        r = step // 4
        v = lax.rem(step, 4)
        for t in range(LATS):
            for j in range(SLOTS):
                base = (t * SLOTS + j) * 7
                planes[step, base : base + 7, :] = four[j, t, pl.ds(pl.multiple_of(step * 8, 8), 8), :][0:7]
        planes[step, 126:128, :] = jnp.zeros((2, LANES), f32)
        return carry

    lax.fori_loop(0, 8, spread, 0)
    for r in range(2):
        for ns in range(2):
            for t in range(LATS):
                for j in range(SLOTS):
                    base = (t * SLOTS + j) * 7 + 6
                    row = 64 + r * 4 + ns
                    planes[r * 4 + ns, base : base + 1, :] = four[j, t, row : row + 1, :]
    for rv in range(8):
        wide[pl.ds(rv, LANES, stride=8), :] = planes[rv].T

    def narrow_one(i, carry):
        rows = pl.ds(pl.multiple_of(i * 128, 128), 128)
        send_one[pl.ds(i * 16, 16)] = wide[rows, :].reshape(16, 8, LANES).astype(bf16)
        return carry

    lax.fori_loop(0, 8, narrow_one, 0)

    def exchange(outgoing, incoming, ssem, rsem):
        pltpu.make_async_copy(outgoing.at[me], incoming.at[me], rsem).start()

        def put(peer):
            pltpu.make_async_remote_copy(
                src_ref=outgoing.at[peer], dst_ref=incoming.at[me], send_sem=ssem, recv_sem=rsem,
                device_id=(peer, lev), device_id_type=MESH,
            ).start()

        put(lax.rem(me + WAVE // 2, WAVE))

        def both(i, carry):
            put(lax.rem(me + WAVE // 2 - i, WAVE))
            put(lax.rem(me + WAVE // 2 + i, WAVE))
            return carry

        lax.fori_loop(1, WAVE // 2, both, 0)

    def settle(outgoing, incoming, ssem, rsem):
        pltpu.make_async_copy(incoming, incoming, rsem).wait()
        part = outgoing.at[pl.ds(0, WAVE - 1)]
        pltpu.make_async_copy(part, part, ssem).wait()

    exchange(send_one, recv_one, ssem_one, rsem_one)

    def level_sum(value, first, second):
        row = lax.broadcasted_iota(jnp.int32, value.shape, 0)
        level = row & 3
        value = value + jnp.where(level >= 1, pltpu.roll(value, 1, 0), 0.0)
        value = value + jnp.where(level >= 2, pltpu.roll(value, 2, 0), 0.0)
        return (value + jnp.where(row < 4, first, second)) * 0.25

    def local(s, carry):
        m = slot_s[me * SLOTS + s]
        row = lax.broadcasted_iota(jnp.int32, (8, LANES), 0)
        live = jnp.where((row < 4) | (m > 0), 1.0, 0.0)
        for t in range(LATS):
            columns = slice(t * LANES, (t + 1) * LANES)
            inside = (2.0 * m.astype(f32) < lat_ref[0:1, columns]).astype(f32)
            for ns in range(2):
                factor = live * (inside * lat_ref[1 + ns : 2 + ns, columns])

                def rows(place, low):
                    return level_sum(
                        four[s, t, pl.ds(place + ns, 8, stride=8), :],
                        four[s, t, low + ns : low + ns + 1, :],
                        four[s, t, low + ns + 4 : low + ns + 5, :],
                    )

                weighted[s, t, ns * 16 + 8 : ns * 16 + 16, :] = rows(2, 66) * factor
                weighted[s, t, 32 + ns * 16 + 8 : 32 + ns * 16 + 16, :] = (
                    four[s, t, pl.ds(6 + ns, 8, stride=8), :] + rows(4, 64)
                ) * factor
        return carry

    lax.fori_loop(0, SLOTS, local, 0)

    settle(send_one, recv_one, ssem_one, rsem_one)

    def widen(incoming):
        def body(i, carry):
            rows = pl.ds(pl.multiple_of(i * 128, 128), 128)
            wide[rows, :] = incoming[pl.ds(i * 16, 16)].astype(f32).reshape(128, LANES)
            return carry

        lax.fori_loop(0, 8, body, 0)
        for rv in range(8):
            planes[rv] = wide[pl.ds(rv, LANES, stride=8), :].T

    widen(recv_one)

    for t in range(LATS):
        points = jnp.full((1, LANES), lon_s[me + LANES * t], jnp.int32)
        for r in range(2):
            for j in range(SLOTS):
                base = (t * SLOTS + j) * 7
                for v in range(4):
                    rv = r * 4 + v
                    pairs[r, j, v * 4 : v * 4 + 4, :] = planes[rv, base : base + 4, :]
                    pairs[r, j, 16 + v * 4 : 18 + v * 4, :] = planes[rv, base + 4 : base + 6, :]
                for ns in range(2):
                    run = planes[r * 4 + ns, base + 6 : base + 7, :]
                    for v in range(4):
                        run = run + planes[r * 4 + v, base + 4 + ns : base + 5 + ns, :]
                        row = 18 + v * 4 + ns
                        pairs[r, j, row : row + 1, :] = run * 0.25
        for q in range(3):
            first = waves_ref[2 * q : 2 * q + 1, :]
            second = waves_ref[2 * q + 1 : 2 * q + 2, :]
            even_first = (first & 1) == 0
            even = jnp.where(even_first, first, second)
            odd = jnp.where(even_first, second, first)
            sigma = 1.0 - (even & 2).astype(f32)
            tau = 1.0 - (odd & 2).astype(f32)
            even_factor = jnp.where(2 * even < points, jnp.where(even == 0, 1.0, 2.0), 0.0)
            odd_factor = jnp.where(2 * odd < points, 2.0, 0.0)
            pick = jnp.broadcast_to(even_first.astype(f32), (32, LANES)) > 0.5
            columns = slice(q * LANES, (q + 1) * LANES)
            real_even = jnp.where(pick, pairs[0, 2 * q], pairs[0, 2 * q + 1]) * even_factor
            real_odd = jnp.where(pick, pairs[0, 2 * q + 1], pairs[0, 2 * q]) * odd_factor
            imag_even = jnp.where(pick, pairs[1, 2 * q], pairs[1, 2 * q + 1]) * even_factor
            imag_odd = jnp.where(pick, pairs[1, 2 * q + 1], pairs[1, 2 * q]) * odd_factor
            left[t, 0, 0:32, columns] = real_even.astype(bf16)
            left[t, 0, 32:64, columns] = (sigma * real_even).astype(bf16)
            left[t, 1, 0:32, columns] = imag_even.astype(bf16)
            left[t, 1, 32:64, columns] = (sigma * imag_even).astype(bf16)
            left[t, 2, 0:32, columns] = real_odd.astype(bf16)
            left[t, 2, 32:64, columns] = (tau * imag_odd).astype(bf16)
            left[t, 3, 0:32, columns] = imag_odd.astype(bf16)
            left[t, 3, 32:64, columns] = (tau * real_odd).astype(bf16)

    def latitude(t, carry):
        whole_points = lon_s[me + LANES * t]
        for i in range(4):
            sumpq[i] = jnp.dot(left[t, i], tables[t, i], preferred_element_type=f32)
        lane = lax.broadcasted_iota(jnp.int32, (1, LANES), 1)
        for block in range(WIDTH // LANES):
            columns = slice(block * LANES, (block + 1) * LANES)
            k = lane + block * LANES
            points = jnp.full((1, LANES), whole_points, jnp.int32)
            share = jnp.where(8 * k < points, 1.0, jnp.where(8 * k == points, 0.5, 0.0))
            share = jnp.where(k == 0, 0.5, share)
            even_p, turn_p = sumpq[0, 0:32, columns], sumpq[0, 32:64, columns]
            even_m, turn_m = sumpq[1, 0:32, columns], sumpq[1, 32:64, columns]
            odd_p, side_m = sumpq[2, 0:32, columns], sumpq[2, 32:64, columns]
            odd_m, side_p = sumpq[3, 0:32, columns], sumpq[3, 32:64, columns]

            def product(grid):
                return grid[0:16] * grid[16:32] * share

            a, b = even_p - even_m, odd_p - odd_m
            f0p, f2p = product(a + b), product(a - b)
            a, b = even_p + even_m, odd_p + odd_m
            f0m, f2m = product(a + b), product(a - b)
            a, b = turn_p - turn_m, side_p + side_m
            f3p, f1p = product(a + b), product(a - b)
            a, b = turn_p + turn_m, side_p - side_m
            f1m, f3m = product(a + b), product(a - b)
            a, b = f0p + f2p, f0m + f2m
            leftback[0, 0:16, columns] = (a + b).astype(bf16)
            leftback[1, 0:16, columns] = (a - b).astype(bf16)
            a, b = f1p + f3p, f1m + f3m
            leftback[0, 16:32, columns] = (a + b).astype(bf16)
            leftback[1, 16:32, columns] = (a - b).astype(bf16)
            a, b = f0p - f2p, f0m - f2m
            leftback[2, 0:16, columns] = (a + b).astype(bf16)
            leftback[3, 0:16, columns] = (a - b).astype(bf16)
            a, b = f1p - f3p, f1m - f3m
            leftback[2, 16:32, columns] = (a + b).astype(bf16)
            leftback[3, 16:32, columns] = (b - a).astype(bf16)
        for i in range(4):
            sumpq[i, 0:32, 0:HALF] = lax.dot_general(
                leftback[i], tables[t, i], (((1,), (1,)), ((), ())), preferred_element_type=f32
            )
        north = quad_s[me + LANES * t]
        south = quad_s[2 * HALF - 1 - me - LANES * t]
        row = lax.broadcasted_iota(jnp.int32, (16, LANES), 0)
        points = jnp.full((1, LANES), whole_points, jnp.int32)
        weight = jnp.where((row & 1) == 0, north, south) * (ROOT / points.astype(f32))
        for q in range(3):
            first = waves_ref[2 * q : 2 * q + 1, :]
            second = waves_ref[2 * q + 1 : 2 * q + 2, :]
            even_first = (first & 1) == 0
            even = jnp.where(even_first, first, second)
            odd = jnp.where(even_first, second, first)
            sigma = 1.0 - (even & 2).astype(f32)
            tau = 1.0 - (odd & 2).astype(f32)
            even_weight = weight * (2 * even < points).astype(f32)
            odd_weight = weight * (2 * odd < points).astype(f32)
            pick = jnp.broadcast_to(even_first.astype(f32), (16, LANES)) > 0.5
            columns = slice(q * LANES, (q + 1) * LANES)
            real_even = (sumpq[0, 0:16, columns] + sigma * sumpq[0, 16:32, columns]) * even_weight
            imag_even = (sumpq[1, 0:16, columns] + sigma * sumpq[1, 16:32, columns]) * -even_weight
            real_odd = (sumpq[2, 0:16, columns] + tau * sumpq[3, 16:32, columns]) * odd_weight
            imag_odd = (sumpq[3, 0:16, columns] + tau * sumpq[2, 16:32, columns]) * -odd_weight
            for r, one, two in ((0, real_even, real_odd), (1, imag_even, imag_odd)):
                for j, value in ((2 * q, jnp.where(pick, one, two)), (2 * q + 1, jnp.where(pick, two, one))):
                    for v in range(4):
                        planes_two[r * 4 + v, t, j * 4 : j * 4 + 4, :] = value[v * 4 : v * 4 + 4]
        return carry

    lax.fori_loop(0, LATS, latitude, 0)

    for rv in range(8):
        filled = planes_two[rv].reshape(LATS * 24, LANES)
        square = jnp.concatenate([filled, jnp.zeros((LANES - LATS * 24, LANES), f32)], axis=0)
        wide[pl.ds(rv, LANES, stride=8), :] = square.T

    def narrow_two(i, carry):
        rows = pl.ds(pl.multiple_of(i * 128, 128), 128)
        send_two[pl.ds(i * 16, 16)] = wide[rows, :].reshape(16, 8, LANES).astype(bf16)
        return carry

    lax.fori_loop(0, 8, narrow_two, 0)
    exchange(send_two, recv_two, ssem_two, rsem_two)
    settle(send_two, recv_two, ssem_two, rsem_two)
    widen(recv_two)
    for rv in range(8):
        for t in range(LATS):
            for j in range(SLOTS):
                base = (t * SLOTS + j) * 4
                weighted[j, t, pl.ds(rv, 4, stride=16), :] = planes[rv, base : base + 4, :]

    def direct(s, carry):
        m = slot_s[me * SLOTS + s]
        keep = (degree >= m).astype(f32) * ROOT
        flipped = keep * (1.0 - 2.0 * ((degree + m) & 1).astype(f32))
        operand = jnp.concatenate([weighted[s, t] for t in range(LATS)], axis=1).astype(bf16)
        product = lax.dot_general(
            operand, legendre_ref[s], (((1,), (1,)), ((), ())), preferred_element_type=f32
        )
        for x in range(2):
            for y in range(2):
                row = x * 32 + y * 8
                value = product[row : row + 8] * keep + product[row + 16 : row + 24] * flipped
                out_ref[s, 0, 2 * x + y] = value[0:4].astype(bf16)
                out_ref[s, 1, 2 * x + y] = value[4:8].astype(bf16)
        return carry

    lax.fori_loop(0, SLOTS, direct, 0)


def per_device(coeffs, legendre, slot_wave, lon_points, quad_weights):
    waves = jnp.pad(slot_wave.reshape(WAVE, SLOTS).T, ((0, 2), (0, 0)))
    latitudes = jnp.stack(
        [lon_points[:HALF].astype(f32), quad_weights[:HALF], quad_weights[HALF:][::-1]], axis=0
    )
    latitudes = jnp.pad(latitudes, ((0, 5), (0, 0)))
    vmem = pl.BlockSpec(memory_space=pltpu.VMEM)
    smem = pl.BlockSpec(memory_space=pltpu.SMEM)
    scratch = [
        pltpu.VMEM((32, DEGREES), f32),
        pltpu.VMEM((32, DEGREES), bf16),
        pltpu.VMEM((LEV, 32, DEGREES), bf16),
        pltpu.VMEM((SLOTS, 8, DEGREES), f32),
        pltpu.VMEM((DEGREES // LANES, 80, LANES), f32),
        pltpu.VMEM((SLOTS, LATS, 80, LANES), f32),
        pltpu.VMEM((6, LANES, LANES), f32),
        pltpu.VMEM((LATS, 4, HALF, WIDTH), bf16),
        pltpu.VMEM((8, LANES, LANES), f32),
        pltpu.VMEM((8 * LANES, LANES), f32),
        pltpu.VMEM((WAVE, 8, LANES), bf16),
        pltpu.VMEM((WAVE, 8, LANES), bf16),
        pltpu.VMEM((WAVE, 8, LANES), bf16),
        pltpu.VMEM((WAVE, 8, LANES), bf16),
        pltpu.VMEM((2, SLOTS, 32, LANES), f32),
        pltpu.VMEM((LATS, 4, 64, HALF), bf16),
        pltpu.VMEM((4, 64, WIDTH), f32),
        pltpu.VMEM((4, 32, WIDTH), bf16),
        pltpu.VMEM((8, LATS, 24, LANES), f32),
        pltpu.VMEM((SLOTS, LATS, 64, LANES), f32),
    ] + [pltpu.SemaphoreType.DMA(())] * 6
    return pl.pallas_call(
        kernel,
        out_shape=jax.ShapeDtypeStruct(coeffs.shape, bf16),
        in_specs=[smem, smem, smem, vmem, vmem, vmem, vmem],
        out_specs=vmem,
        scratch_shapes=scratch,
        compiler_params=pltpu.CompilerParams(
            collective_id=0, has_side_effects=True, vmem_limit_bytes=48 * 1024 * 1024
        ),
    )(lon_points, slot_wave, quad_weights, waves, latitudes, coeffs, legendre)


def solution(mesh):
    placed = (P("wave", None, None, "lev", None), P("wave", None, None), P(), P(), P())
    return jax.shard_map(
        per_device,
        mesh=mesh,
        in_specs=placed,
        out_specs=P("wave", None, None, "lev", None),
        check_vma=False,
    )
```

```python
import math

import numpy as np
import jax
import jax.numpy as jnp
from jax import lax
from jax.experimental import pallas as pl
from jax.experimental.pallas import tpu as pltpu
from jax.sharding import PartitionSpec as P

MESH = pl.DeviceIdType.MESH
f32 = jnp.float32
bf16 = jnp.bfloat16
SLOTS = 6
DEGREES = 768
HALF = 384
WAVE = 128
LEV = 4
LATS = 3
LANES = 128
WIDTH = 512
ROOT = 1.0 / math.sqrt(768.0)


def turn_polynomials(terms):
    x = np.cos(np.linspace(0.0, np.pi, 4001)) * 0.5
    y = x * x
    powers = np.stack([y**i for i in range(terms)], axis=1)
    cosine = np.linalg.lstsq(powers, np.cos(2 * np.pi * x), rcond=None)[0]
    sine = np.linalg.lstsq(powers * x[:, None], np.sin(2 * np.pi * x), rcond=None)[0]
    return [float(np.float32(c)) for c in cosine], [float(np.float32(c)) for c in sine]


COSINE, SINE = turn_polynomials(6)


def horner(coefficients, y):
    total = coefficients[-1]
    for c in coefficients[-2::-1]:
        total = total * y + c
    return total


def kernel(
    lon_h, slot_h, quad_h, coeffs_h, legendre_h, out_ref,
    lon_s, slot_s, quad_s, lon_v, slot_v, quad_v, coeffs_ref, legendre_ref, waves_ref, lat_ref,
    sums, lev_send, lev_recv, lower, stage, four, column, tables, planes, wide,
    send_one, recv_one, send_two, recv_two, pairs, left, sumpq, leftback, planes_two, weighted,
    mass_sums, mass_send, mass_recv, mass_lower, low_four,
    small_sem, coeffs_sem, legendre_sem,
    lev_ssem, lev_rsem, mass_ssem, mass_rsem, ssem_one, rsem_one, ssem_two, rsem_two,
):
    me = lax.axis_index("wave")
    lev = lax.axis_index("lev")
    barrier = pltpu.get_barrier_semaphore()
    small = [
        pltpu.make_async_copy(src, dst, small_sem.at[i])
        for i, (src, dst) in enumerate(
            ((slot_h, slot_s), (lon_h, lon_s), (quad_h, quad_s), (slot_h, slot_v), (lon_h, lon_v), (quad_h, quad_v))
        )
    ]
    load_coeffs = pltpu.make_async_copy(coeffs_h, coeffs_ref, coeffs_sem)

    def load_legendre(s):
        return pltpu.make_async_copy(legendre_h.at[s], legendre_ref.at[s], legendre_sem.at[s])

    small[0].start()
    load_coeffs.start()
    for s in range(SLOTS):
        load_legendre(s).start()
    for copy in small[1:]:
        copy.start()
    for i in range(1, LEV):
        pl.semaphore_signal(barrier, inc=1, device_id=(me, lax.rem(lev + i, LEV)), device_id_type=MESH)

    def greet(i, carry):
        pl.semaphore_signal(barrier, inc=1, device_id=(lax.rem(me + i, WAVE), lev), device_id_type=MESH)
        return carry

    lax.fori_loop(1, WAVE, greet, 0)
    small[0].wait()
    load_coeffs.wait()

    degree = lax.broadcasted_iota(jnp.int32, (1, DEGREES), 1)
    place = (0, 4, 2, 6)

    def put_rows(start, stride, value):
        for b in range(DEGREES // LANES):
            stage[b, pl.ds(start, 4, stride=stride), :] = value[:, b * LANES : (b + 1) * LANES]

    def forward(s, carry):
        load_legendre(s).wait()
        m = slot_s[me * SLOTS + s]
        keep = (degree >= m).astype(f32)
        flipped = keep * (1.0 - 2.0 * ((degree + m) & 1).astype(f32))
        for r in range(2):
            for f in range(4):
                value = coeffs_ref[s, r, f].astype(f32)
                put_rows(r * 32 + place[f], 8, value * keep)
                put_rows(r * 32 + place[f] + 1, 8, value * flipped)
        operand = jnp.concatenate([stage[b] for b in range(DEGREES // LANES)], axis=1).astype(bf16)
        product = jnp.dot(operand, legendre_ref[s], preferred_element_type=f32) * ROOT
        for t in range(LATS):
            four[s, t] = product[:, t * LANES : (t + 1) * LANES]
        return carry

    lax.fori_loop(0, SLOTS, forward, 0)

    sums[24:32, :] = jnp.zeros((8, DEGREES), f32)
    for s in range(SLOTS):
        for r in range(2):
            for f in (1, 2):
                row = s * 4 + r * 2 + f - 1
                sums[row : row + 1, :] = jnp.sum(coeffs_ref[s, r, f].astype(f32), axis=0, keepdims=True)
    lev_send[...] = sums[...].astype(bf16)

    def to_levels(outgoing, incoming, ssem, rsem):
        for i in range(1, LEV):
            pltpu.make_async_remote_copy(
                src_ref=outgoing, dst_ref=incoming.at[lev], send_sem=ssem, recv_sem=rsem,
                device_id=(me, lax.rem(lev + i, LEV)), device_id_type=MESH,
            ).start()

    def from_levels(outgoing, incoming, ssem, rsem):
        part = incoming.at[pl.ds(0, LEV - 1)]
        pltpu.make_async_copy(part, part, rsem).wait()
        pltpu.make_async_copy(part, part, ssem).wait()
        total = jnp.zeros(outgoing.shape, f32)
        for k in range(LEV):
            total = total + jnp.where(k < lev, incoming[k].astype(f32), 0.0)
        return total

    def spread(step, carry):
        planes[step, 104:128, :] = jnp.zeros((24, LANES), f32)
        for t in range(LATS):
            for j in range(SLOTS):
                base = (t * SLOTS + j) * 6
                planes[step, base : base + 6, :] = four[j, t, pl.ds(pl.multiple_of(step * 8, 8), 8), :][0:6]
        return carry

    lax.fori_loop(0, 8, spread, 0)
    for rv in range(8):
        wide[pl.ds(rv, LANES, stride=8), :] = planes[rv].T

    def narrow_one(i, carry):
        rows = pl.ds(pl.multiple_of(i * 128, 128), 128)
        send_one[pl.ds(i * 16, 16)] = wide[rows, :].reshape(16, 8, LANES).astype(bf16)
        return carry

    lax.fori_loop(0, 8, narrow_one, 0)

    def exchange(outgoing, incoming, ssem, rsem):
        pltpu.make_async_copy(outgoing.at[me], incoming.at[me], rsem).start()

        def put(peer):
            pltpu.make_async_remote_copy(
                src_ref=outgoing.at[peer], dst_ref=incoming.at[me], send_sem=ssem, recv_sem=rsem,
                device_id=(peer, lev), device_id_type=MESH,
            ).start()

        put(lax.rem(me + WAVE // 2, WAVE))

        def both(i, carry):
            put(lax.rem(me + WAVE // 2 - i, WAVE))
            put(lax.rem(me + WAVE // 2 + i, WAVE))
            return carry

        lax.fori_loop(1, WAVE // 2, both, 0)

    def settle(outgoing, incoming, ssem, rsem):
        pltpu.make_async_copy(incoming, incoming, rsem).wait()
        part = outgoing.at[pl.ds(0, WAVE - 1)]
        pltpu.make_async_copy(part, part, ssem).wait()

    lev_recv[lev] = jnp.zeros((32, DEGREES), bf16)
    mass_recv[lev] = jnp.zeros((SLOTS, 16, LANES), bf16)
    pl.semaphore_wait(barrier, WAVE - 1 + LEV - 1)
    exchange(send_one, recv_one, ssem_one, rsem_one)
    to_levels(lev_send, lev_recv, lev_ssem, lev_rsem)
    for copy in small[1:]:
        copy.wait()

    number = lax.broadcasted_iota(jnp.int32, (8, DEGREES), 1).astype(f32)
    group = jnp.floor((number + 0.5) * (1.0 / SLOTS))
    mine = (number - group * SLOTS) == lax.broadcasted_iota(jnp.int32, (8, DEGREES), 0).astype(f32)
    every = jnp.concatenate([slot_v[pl.ds(b * LANES, LANES)].reshape(1, LANES) for b in range(6)], axis=1)
    high = jnp.where(mine, (every >> 4).astype(f32), 0.0)
    low = jnp.where(mine, (every & 15).astype(f32), 0.0)
    ahead = lax.broadcasted_iota(jnp.int32, (DEGREES, LANES), 0) - SLOTS * lax.broadcasted_iota(
        jnp.int32, (DEGREES, LANES), 1
    )
    belongs = jnp.where((ahead >= 0) & (ahead < SLOTS), 1.0, 0.0).astype(bf16)
    split = jnp.dot(
        jnp.concatenate([high, low], axis=0).astype(bf16), belongs, preferred_element_type=f32
    )
    waves_ref[...] = (split[0:8] * 16.0 + split[8:16]).astype(jnp.int32)
    flip = lax.broadcasted_iota(jnp.int32, (LANES, LANES), 0) + lax.broadcasted_iota(jnp.int32, (LANES, LANES), 1)
    flip = jnp.where(flip == LANES - 1, 1.0, 0.0)
    for t in range(LATS):
        south = jnp.broadcast_to(quad_v[pl.ds((5 - t) * LANES, LANES)].reshape(1, LANES), (8, LANES))
        south = jnp.dot(south, flip, preferred_element_type=f32, precision=lax.Precision.HIGHEST)
        lat_ref[t, 0:1, :] = lon_v[pl.ds(t * LANES, LANES)].reshape(1, LANES).astype(f32)
        lat_ref[t, 1:2, :] = quad_v[pl.ds(t * LANES, LANES)].reshape(1, LANES)
        lat_ref[t, 2:3, :] = south[0:1]

    for q in range(3):
        first = waves_ref[2 * q : 2 * q + 1, :]
        second = waves_ref[2 * q + 1 : 2 * q + 2, :]
        even_first = (first & 1) == 0
        even = jnp.where(even_first, first, second)
        odd = jnp.where(even_first, second, first)
        column[q] = jnp.broadcast_to(even.astype(f32), (LANES, LANES)).T
        column[3 + q] = jnp.broadcast_to(odd.astype(f32), (LANES, LANES)).T

    def table_block(step, carry):
        t = step // 6
        c = lax.rem(step, 6)
        parity = c // 3
        q = lax.rem(c, 3)
        points = lon_s[me + LANES * t]
        per_point = 1.0 / jnp.full((1, LANES), points, jnp.int32).astype(f32)
        wave = column[c]
        lane = lax.broadcasted_iota(jnp.int32, (1, LANES), 1).astype(f32)
        for block in range(WIDTH // LANES):
            turn = wave * (lane + float(block * LANES)) * per_point
            x = turn - jnp.floor(turn + 0.5)
            y = x * x
            rows = pl.ds(pl.multiple_of(q * LANES, LANES), LANES)
            columns = pl.ds(block * LANES, LANES)
            tables[t, 2 * parity, rows, columns] = horner(COSINE, y).astype(bf16)
            tables[t, 2 * parity + 1, rows, columns] = (horner(SINE, y) * x).astype(bf16)
        return carry

    lax.fori_loop(0, 2 * 6, table_block, 0)

    settle(send_one, recv_one, ssem_one, rsem_one)

    def widen(incoming):
        def body(i, carry):
            rows = pl.ds(pl.multiple_of(i * 128, 128), 128)
            wide[rows, :] = incoming[pl.ds(i * 16, 16)].astype(f32).reshape(128, LANES)
            return carry

        lax.fori_loop(0, 8, body, 0)
        for rv in range(8):
            planes[rv] = wide[pl.ds(rv, LANES, stride=8), :].T

    widen(recv_one)

    mass_sums[...] = jnp.zeros((SLOTS, 16, LANES), f32)
    for t in range(LATS):
        for j in range(SLOTS):
            base = (t * SLOTS + j) * 6 + 4
            for r in range(2):
                value = planes[r * 4, base : base + 2, :]
                for v in range(1, 4):
                    value = value + planes[r * 4 + v, base : base + 2, :]
                row = r * 6 + t * 2
                mass_sums[j, row : row + 2, :] = value
    mass_send[...] = mass_sums[...].astype(bf16)
    to_levels(mass_send, mass_recv, mass_ssem, mass_rsem)
    lax.fori_loop(2 * 6, LATS * 6, table_block, 0)

    for t in range(LATS):
        for r in range(2):
            for j in range(SLOTS):
                base = (t * SLOTS + j) * 6
                for v in range(4):
                    rv = r * 4 + v
                    pairs[t, r, j, v * 4 : v * 4 + 4, :] = planes[rv, base : base + 4, :]
                    pairs[t, r, j, 16 + v * 4 : 18 + v * 4, :] = planes[rv, base + 4 : base + 6, :]
    mass_lower[...] = from_levels(mass_send, mass_recv, mass_ssem, mass_rsem)
    for t in range(LATS):
        points = jnp.full((1, LANES), lon_s[me + LANES * t], jnp.int32)
        for r in range(2):
            for j in range(SLOTS):
                base = (t * SLOTS + j) * 6 + 4
                row = r * 6 + t * 2
                run = mass_lower[j, row : row + 2, :]
                for v in range(4):
                    run = run + planes[r * 4 + v, base : base + 2, :]
                    pairs[t, r, j, 18 + v * 4 : 20 + v * 4, :] = run * 0.25
        for q in range(3):
            first = waves_ref[2 * q : 2 * q + 1, :]
            second = waves_ref[2 * q + 1 : 2 * q + 2, :]
            even_first = (first & 1) == 0
            even = jnp.where(even_first, first, second)
            odd = jnp.where(even_first, second, first)
            sigma = 1.0 - (even & 2).astype(f32)
            tau = 1.0 - (odd & 2).astype(f32)
            even_factor = jnp.where(2 * even < points, jnp.where(even == 0, 1.0, 2.0), 0.0)
            odd_factor = jnp.where(2 * odd < points, 2.0, 0.0)
            pick = jnp.broadcast_to(even_first.astype(f32), (32, LANES)) > 0.5
            columns = slice(q * LANES, (q + 1) * LANES)
            real_even = jnp.where(pick, pairs[t, 0, 2 * q], pairs[t, 0, 2 * q + 1]) * even_factor
            real_odd = jnp.where(pick, pairs[t, 0, 2 * q + 1], pairs[t, 0, 2 * q]) * odd_factor
            imag_even = jnp.where(pick, pairs[t, 1, 2 * q], pairs[t, 1, 2 * q + 1]) * even_factor
            imag_odd = jnp.where(pick, pairs[t, 1, 2 * q + 1], pairs[t, 1, 2 * q]) * odd_factor
            left[t, 0, 0:32, columns] = real_even.astype(bf16)
            left[t, 0, 32:64, columns] = (sigma * real_even).astype(bf16)
            left[t, 1, 0:32, columns] = imag_even.astype(bf16)
            left[t, 1, 32:64, columns] = (sigma * imag_even).astype(bf16)
            left[t, 2, 0:32, columns] = real_odd.astype(bf16)
            left[t, 2, 32:64, columns] = (tau * imag_odd).astype(bf16)
            left[t, 3, 0:32, columns] = imag_odd.astype(bf16)
            left[t, 3, 32:64, columns] = (tau * real_odd).astype(bf16)

    def latitude(t, carry):
        whole_points = lon_s[me + LANES * t]
        for i in range(4):
            sumpq[i] = jnp.dot(left[t, i], tables[t, i], preferred_element_type=f32)
        lane = lax.broadcasted_iota(jnp.int32, (1, LANES), 1)
        for block in range(WIDTH // LANES):
            columns = slice(block * LANES, (block + 1) * LANES)
            k = lane + block * LANES
            points = jnp.full((1, LANES), whole_points, jnp.int32)
            share = jnp.where(8 * k < points, 1.0, jnp.where(8 * k == points, 0.5, 0.0))
            share = jnp.where(k == 0, 0.5, share)
            even_p, turn_p = sumpq[0, 0:32, columns], sumpq[0, 32:64, columns]
            even_m, turn_m = sumpq[1, 0:32, columns], sumpq[1, 32:64, columns]
            odd_p, side_m = sumpq[2, 0:32, columns], sumpq[2, 32:64, columns]
            odd_m, side_p = sumpq[3, 0:32, columns], sumpq[3, 32:64, columns]

            def product(grid):
                return grid[0:16] * grid[16:32] * share

            a, b = even_p - even_m, odd_p - odd_m
            f0p, f2p = product(a + b), product(a - b)
            a, b = even_p + even_m, odd_p + odd_m
            f0m, f2m = product(a + b), product(a - b)
            a, b = turn_p - turn_m, side_p + side_m
            f3p, f1p = product(a + b), product(a - b)
            a, b = turn_p + turn_m, side_p - side_m
            f1m, f3m = product(a + b), product(a - b)
            a, b = f0p + f2p, f0m + f2m
            leftback[0, 0:16, columns] = (a + b).astype(bf16)
            leftback[1, 0:16, columns] = (a - b).astype(bf16)
            a, b = f1p + f3p, f1m + f3m
            leftback[0, 16:32, columns] = (a + b).astype(bf16)
            leftback[1, 16:32, columns] = (a - b).astype(bf16)
            a, b = f0p - f2p, f0m - f2m
            leftback[2, 0:16, columns] = (a + b).astype(bf16)
            leftback[3, 0:16, columns] = (a - b).astype(bf16)
            a, b = f1p - f3p, f1m - f3m
            leftback[2, 16:32, columns] = (a + b).astype(bf16)
            leftback[3, 16:32, columns] = (b - a).astype(bf16)
        for i in range(4):
            sumpq[i, 0:32, 0:HALF] = lax.dot_general(
                leftback[i], tables[t, i], (((1,), (1,)), ((), ())), preferred_element_type=f32
            )
        north = quad_s[me + LANES * t]
        south = quad_s[2 * HALF - 1 - me - LANES * t]
        row = lax.broadcasted_iota(jnp.int32, (16, LANES), 0)
        points = jnp.full((1, LANES), whole_points, jnp.int32)
        weight = jnp.where((row & 1) == 0, north, south) * (ROOT / points.astype(f32))
        for q in range(3):
            first = waves_ref[2 * q : 2 * q + 1, :]
            second = waves_ref[2 * q + 1 : 2 * q + 2, :]
            even_first = (first & 1) == 0
            even = jnp.where(even_first, first, second)
            odd = jnp.where(even_first, second, first)
            sigma = 1.0 - (even & 2).astype(f32)
            tau = 1.0 - (odd & 2).astype(f32)
            even_weight = weight * (2 * even < points).astype(f32)
            odd_weight = weight * (2 * odd < points).astype(f32)
            pick = jnp.broadcast_to(even_first.astype(f32), (16, LANES)) > 0.5
            columns = slice(q * LANES, (q + 1) * LANES)
            real_even = (sumpq[0, 0:16, columns] + sigma * sumpq[0, 16:32, columns]) * even_weight
            imag_even = (sumpq[1, 0:16, columns] + sigma * sumpq[1, 16:32, columns]) * -even_weight
            real_odd = (sumpq[2, 0:16, columns] + tau * sumpq[3, 16:32, columns]) * odd_weight
            imag_odd = (sumpq[3, 0:16, columns] + tau * sumpq[2, 16:32, columns]) * -odd_weight
            for r, one, two in ((0, real_even, real_odd), (1, imag_even, imag_odd)):
                for j, value in ((2 * q, jnp.where(pick, one, two)), (2 * q + 1, jnp.where(pick, two, one))):
                    for v in range(4):
                        planes_two[r * 4 + v, t, j * 4 : j * 4 + 4, :] = value[v * 4 : v * 4 + 4]
        return carry

    lax.fori_loop(0, LATS, latitude, 0)

    for rv in range(8):
        filled = planes_two[rv].reshape(LATS * 24, LANES)
        square = jnp.concatenate([filled, jnp.zeros((LANES - LATS * 24, LANES), f32)], axis=0)
        wide[pl.ds(rv, LANES, stride=8), :] = square.T

    def narrow_two(i, carry):
        rows = pl.ds(pl.multiple_of(i * 128, 128), 128)
        send_two[pl.ds(i * 16, 16)] = wide[rows, :].reshape(16, 8, LANES).astype(bf16)
        return carry

    lax.fori_loop(0, 8, narrow_two, 0)
    exchange(send_two, recv_two, ssem_two, rsem_two)
    def level_sum(value, first, second):
        row = lax.broadcasted_iota(jnp.int32, value.shape, 0)
        level = row & 3
        value = value + jnp.where(level >= 1, pltpu.roll(value, 1, 0), 0.0)
        value = value + jnp.where(level >= 2, pltpu.roll(value, 2, 0), 0.0)
        return (value + jnp.where(row < 4, first, second)) * 0.25

    def local(s, carry):
        m = slot_s[me * SLOTS + s]
        keep = (degree >= m).astype(f32)
        flipped = keep * (1.0 - 2.0 * ((degree + m) & 1).astype(f32))
        side = lax.broadcasted_iota(jnp.int32, (8, DEGREES), 0)
        extra = lower[s] * jnp.where(side < 4, keep, flipped)
        extra = jnp.concatenate([extra, jnp.zeros((8, DEGREES), f32)], axis=0).astype(bf16)
        product = jnp.dot(extra, legendre_ref[s], preferred_element_type=f32) * ROOT
        for t in range(LATS):
            low_four[t] = product[0:8, t * LANES : (t + 1) * LANES]
        row = lax.broadcasted_iota(jnp.int32, (8, LANES), 0)
        live = jnp.where((row < 4) | (m > 0), 1.0, 0.0)
        for t in range(LATS):
            inside = (2.0 * m.astype(f32) < lat_ref[t, 0:1, :]).astype(f32)
            for ns in range(2):
                factor = live * (inside * lat_ref[t, 1 + ns : 2 + ns, :])

                def rows(place, low):
                    return level_sum(
                        four[s, t, pl.ds(place + ns, 8, stride=8), :],
                        low_four[t, 4 * ns + low : 4 * ns + low + 1, :],
                        low_four[t, 4 * ns + low + 2 : 4 * ns + low + 3, :],
                    )

                weighted[s, t, ns * 16 + 8 : ns * 16 + 16, :] = rows(2, 1) * factor
                weighted[s, t, 32 + ns * 16 + 8 : 32 + ns * 16 + 16, :] = (
                    four[s, t, pl.ds(6 + ns, 8, stride=8), :] + rows(4, 0)
                ) * factor
        return carry

    total = from_levels(lev_send, lev_recv, lev_ssem, lev_rsem)
    sums[...] = total
    for s in range(SLOTS):
        lower[s, 0:4, :] = sums[s * 4 : s * 4 + 4, :]
        lower[s, 4:8, :] = sums[s * 4 : s * 4 + 4, :]
    lax.fori_loop(0, SLOTS, local, 0)

    settle(send_two, recv_two, ssem_two, rsem_two)
    widen(recv_two)
    for rv in range(8):
        for t in range(LATS):
            for j in range(SLOTS):
                base = (t * SLOTS + j) * 4
                weighted[j, t, pl.ds(rv, 4, stride=16), :] = planes[rv, base : base + 4, :]

    def direct(s, carry):
        m = slot_s[me * SLOTS + s]
        keep = (degree >= m).astype(f32) * ROOT
        flipped = keep * (1.0 - 2.0 * ((degree + m) & 1).astype(f32))
        operand = jnp.concatenate([weighted[s, t] for t in range(LATS)], axis=1).astype(bf16)
        product = lax.dot_general(
            operand, legendre_ref[s], (((1,), (1,)), ((), ())), preferred_element_type=f32
        )
        for x in range(2):
            for y in range(2):
                row = x * 32 + y * 8
                value = product[row : row + 8] * keep + product[row + 16 : row + 24] * flipped
                out_ref[s, 0, 2 * x + y] = value[0:4].astype(bf16)
                out_ref[s, 1, 2 * x + y] = value[4:8].astype(bf16)
        return carry

    lax.fori_loop(0, SLOTS, direct, 0)


def per_device(coeffs, legendre, slot_wave, lon_points, quad_weights):
    vmem = pl.BlockSpec(memory_space=pltpu.VMEM)
    outside = pl.BlockSpec(memory_space=pltpu.HBM)
    scratch = [
        pltpu.SMEM((DEGREES,), jnp.int32),
        pltpu.SMEM((DEGREES,), jnp.int32),
        pltpu.SMEM((DEGREES,), f32),
        pltpu.VMEM((DEGREES,), jnp.int32),
        pltpu.VMEM((DEGREES,), jnp.int32),
        pltpu.VMEM((DEGREES,), f32),
        pltpu.VMEM(coeffs.shape, bf16),
        pltpu.VMEM(legendre.shape, bf16),
        pltpu.VMEM((8, LANES), jnp.int32),
        pltpu.VMEM((LATS, 8, LANES), f32),
        pltpu.VMEM((32, DEGREES), f32),
        pltpu.VMEM((32, DEGREES), bf16),
        pltpu.VMEM((LEV, 32, DEGREES), bf16),
        pltpu.VMEM((SLOTS, 8, DEGREES), f32),
        pltpu.VMEM((DEGREES // LANES, 64, LANES), f32),
        pltpu.VMEM((SLOTS, LATS, 64, LANES), f32),
        pltpu.VMEM((6, LANES, LANES), f32),
        pltpu.VMEM((LATS, 4, HALF, WIDTH), bf16),
        pltpu.VMEM((8, LANES, LANES), f32),
        pltpu.VMEM((8 * LANES, LANES), f32),
        pltpu.VMEM((WAVE, 8, LANES), bf16),
        pltpu.VMEM((WAVE, 8, LANES), bf16),
        pltpu.VMEM((WAVE, 8, LANES), bf16),
        pltpu.VMEM((WAVE, 8, LANES), bf16),
        pltpu.VMEM((LATS, 2, SLOTS, 32, LANES), f32),
        pltpu.VMEM((LATS, 4, 64, HALF), bf16),
        pltpu.VMEM((4, 64, WIDTH), f32),
        pltpu.VMEM((4, 32, WIDTH), bf16),
        pltpu.VMEM((8, LATS, 24, LANES), f32),
        pltpu.VMEM((SLOTS, LATS, 64, LANES), f32),
        pltpu.VMEM((SLOTS, 16, LANES), f32),
        pltpu.VMEM((SLOTS, 16, LANES), bf16),
        pltpu.VMEM((LEV, SLOTS, 16, LANES), bf16),
        pltpu.VMEM((SLOTS, 16, LANES), f32),
        pltpu.VMEM((LATS, 8, LANES), f32),
        pltpu.SemaphoreType.DMA((6,)),
        pltpu.SemaphoreType.DMA(()),
        pltpu.SemaphoreType.DMA((SLOTS,)),
    ] + [pltpu.SemaphoreType.DMA(())] * 8
    return pl.pallas_call(
        kernel,
        out_shape=jax.ShapeDtypeStruct(coeffs.shape, bf16),
        in_specs=[outside] * 5,
        out_specs=vmem,
        scratch_shapes=scratch,
        compiler_params=pltpu.CompilerParams(
            collective_id=0, has_side_effects=True, vmem_limit_bytes=63 * 1024 * 1024
        ),
    )(lon_points, slot_wave, quad_weights, coeffs, legendre)


def solution(mesh):
    placed = (P("wave", None, None, "lev", None), P("wave", None, None), P(), P(), P())
    return jax.shard_map(
        per_device,
        mesh=mesh,
        in_specs=placed,
        out_specs=P("wave", None, None, "lev", None),
        check_vma=False,
    )
```

```python
import math

import numpy as np
import jax
import jax.numpy as jnp
from jax import lax
from jax.experimental import pallas as pl
from jax.experimental.pallas import tpu as pltpu
from jax.sharding import PartitionSpec as P

MESH = pl.DeviceIdType.MESH
f32 = jnp.float32
bf16 = jnp.bfloat16
SLOTS = 6
DEGREES = 768
HALF = 384
WAVE = 128
LEV = 4
LATS = 3
LANES = 128
WIDTH = 512
ROOT = 1.0 / math.sqrt(768.0)


def turn_polynomials(terms):
    x = np.cos(np.linspace(0.0, np.pi, 4001)) * 0.5
    y = x * x
    powers = np.stack([y**i for i in range(terms)], axis=1)
    cosine = np.linalg.lstsq(powers, np.cos(2 * np.pi * x), rcond=None)[0]
    sine = np.linalg.lstsq(powers * x[:, None], np.sin(2 * np.pi * x), rcond=None)[0]
    return [float(np.float32(c)) for c in cosine], [float(np.float32(c)) for c in sine]


COSINE, SINE = turn_polynomials(6)


def horner(coefficients, y):
    total = coefficients[-1]
    for c in coefficients[-2::-1]:
        total = total * y + c
    return total


def kernel(
    lon_h, slot_h, quad_h, coeffs_h, legendre_h, out_ref,
    lon_s, slot_s, quad_s, lon_v, slot_v, quad_v, coeffs_ref, legendre_ref, waves_ref, lat_ref,
    sums, lev_send, lev_recv, lower, stage, four, column, tables, planes, wide,
    send_one, recv_one, send_two, recv_two, pairs, left, sumpq, leftback, planes_two, weighted,
    mass_sums, mass_send, mass_recv, mass_lower, low_four,
    small_sem, coeffs_sem, legendre_sem,
    lev_ssem, lev_rsem, mass_ssem, mass_rsem, ssem_one, rsem_one, ssem_two, rsem_two,
):
    me = lax.axis_index("wave")
    lev = lax.axis_index("lev")
    barrier = pltpu.get_barrier_semaphore()
    small = [
        pltpu.make_async_copy(src, dst, small_sem.at[i])
        for i, (src, dst) in enumerate(
            ((slot_h, slot_s), (lon_h, lon_s), (quad_h, quad_s), (slot_h, slot_v), (lon_h, lon_v), (quad_h, quad_v))
        )
    ]
    load_coeffs = pltpu.make_async_copy(coeffs_h, coeffs_ref, coeffs_sem)

    def load_legendre(s):
        return pltpu.make_async_copy(legendre_h.at[s], legendre_ref.at[s], legendre_sem.at[s])

    small[0].start()
    load_coeffs.start()
    for s in range(SLOTS):
        load_legendre(s).start()
    for copy in small[1:]:
        copy.start()
    for i in range(1, LEV):
        pl.semaphore_signal(barrier, inc=1, device_id=(me, lax.rem(lev + i, LEV)), device_id_type=MESH)

    def greet(i, carry):
        pl.semaphore_signal(barrier, inc=1, device_id=(lax.rem(me + i, WAVE), lev), device_id_type=MESH)
        return carry

    lax.fori_loop(1, WAVE, greet, 0)
    small[0].wait()
    load_coeffs.wait()

    degree = lax.broadcasted_iota(jnp.int32, (1, DEGREES), 1)
    place = (0, 4, 2, 6)

    def put_rows(start, stride, value):
        for b in range(DEGREES // LANES):
            stage[b, pl.ds(start, 4, stride=stride), :] = value[:, b * LANES : (b + 1) * LANES]

    def forward(s, carry):
        load_legendre(s).wait()
        m = slot_s[me * SLOTS + s]
        keep = (degree >= m).astype(f32)
        flipped = keep * (1.0 - 2.0 * ((degree + m) & 1).astype(f32))
        for r in range(2):
            for f in range(4):
                value = coeffs_ref[s, r, f].astype(f32)
                put_rows(r * 32 + place[f], 8, value * keep)
                put_rows(r * 32 + place[f] + 1, 8, value * flipped)
        operand = jnp.concatenate([stage[b] for b in range(DEGREES // LANES)], axis=1).astype(bf16)
        product = jnp.dot(operand, legendre_ref[s], preferred_element_type=f32) * ROOT
        for t in range(LATS):
            four[s, t] = product[:, t * LANES : (t + 1) * LANES]
        return carry

    lax.fori_loop(0, SLOTS, forward, 0)

    sums[24:32, :] = jnp.zeros((8, DEGREES), f32)
    for s in range(SLOTS):
        for r in range(2):
            for f in (1, 2):
                row = s * 4 + r * 2 + f - 1
                sums[row : row + 1, :] = jnp.sum(coeffs_ref[s, r, f].astype(f32), axis=0, keepdims=True)
    lev_send[...] = sums[...].astype(bf16)

    def to_levels(outgoing, incoming, ssem, rsem):
        for i in range(1, LEV):
            pltpu.make_async_remote_copy(
                src_ref=outgoing, dst_ref=incoming.at[lev], send_sem=ssem, recv_sem=rsem,
                device_id=(me, lax.rem(lev + i, LEV)), device_id_type=MESH,
            ).start()

    def from_levels(outgoing, incoming, ssem, rsem):
        part = incoming.at[pl.ds(0, LEV - 1)]
        pltpu.make_async_copy(part, part, rsem).wait()
        pltpu.make_async_copy(part, part, ssem).wait()
        total = jnp.zeros(outgoing.shape, f32)
        for k in range(LEV):
            total = total + jnp.where(k < lev, incoming[k].astype(f32), 0.0)
        return total

    def spread(step, carry):
        planes[step, 104:128, :] = jnp.zeros((24, LANES), f32)
        for t in range(LATS):
            for j in range(SLOTS):
                base = (t * SLOTS + j) * 6
                planes[step, base : base + 6, :] = four[j, t, pl.ds(pl.multiple_of(step * 8, 8), 8), :][0:6]
        return carry

    lax.fori_loop(0, 8, spread, 0)
    for rv in range(8):
        wide[pl.ds(rv, LANES, stride=8), :] = planes[rv].T

    def narrow_one(i, carry):
        rows = pl.ds(pl.multiple_of(i * 128, 128), 128)
        send_one[pl.ds(i * 16, 16)] = wide[rows, :].reshape(16, 8, LANES).astype(bf16)
        return carry

    lax.fori_loop(0, 8, narrow_one, 0)

    def exchange(outgoing, incoming, ssem, rsem):
        pltpu.make_async_copy(outgoing.at[me], incoming.at[me], rsem).start()

        def put(peer):
            pltpu.make_async_remote_copy(
                src_ref=outgoing.at[peer], dst_ref=incoming.at[me], send_sem=ssem, recv_sem=rsem,
                device_id=(peer, lev), device_id_type=MESH,
            ).start()

        put(lax.rem(me + WAVE // 2, WAVE))

        def both(i, carry):
            put(lax.rem(me + WAVE // 2 - i, WAVE))
            put(lax.rem(me + WAVE // 2 + i, WAVE))
            return carry

        lax.fori_loop(1, WAVE // 2, both, 0)

    def settle(outgoing, incoming, ssem, rsem):
        pltpu.make_async_copy(incoming, incoming, rsem).wait()
        part = outgoing.at[pl.ds(0, WAVE - 1)]
        pltpu.make_async_copy(part, part, ssem).wait()

    lev_recv[lev] = jnp.zeros((32, DEGREES), bf16)
    mass_recv[lev] = jnp.zeros((SLOTS, 16, LANES), bf16)
    pl.semaphore_wait(barrier, WAVE - 1 + LEV - 1)
    exchange(send_one, recv_one, ssem_one, rsem_one)
    to_levels(lev_send, lev_recv, lev_ssem, lev_rsem)
    for copy in small[1:]:
        copy.wait()

    planes_two[:, :, 96:LANES, :] = jnp.zeros((LATS, 2, LANES - 96, LANES), f32)

    number = lax.broadcasted_iota(jnp.int32, (8, DEGREES), 1).astype(f32)
    group = jnp.floor((number + 0.5) * (1.0 / SLOTS))
    mine = (number - group * SLOTS) == lax.broadcasted_iota(jnp.int32, (8, DEGREES), 0).astype(f32)
    every = jnp.concatenate([slot_v[pl.ds(b * LANES, LANES)].reshape(1, LANES) for b in range(6)], axis=1)
    high = jnp.where(mine, (every >> 4).astype(f32), 0.0)
    low = jnp.where(mine, (every & 15).astype(f32), 0.0)
    ahead = lax.broadcasted_iota(jnp.int32, (DEGREES, LANES), 0) - SLOTS * lax.broadcasted_iota(
        jnp.int32, (DEGREES, LANES), 1
    )
    belongs = jnp.where((ahead >= 0) & (ahead < SLOTS), 1.0, 0.0).astype(bf16)
    split = jnp.dot(
        jnp.concatenate([high, low], axis=0).astype(bf16), belongs, preferred_element_type=f32
    )
    waves_ref[...] = (split[0:8] * 16.0 + split[8:16]).astype(jnp.int32)
    flip = lax.broadcasted_iota(jnp.int32, (LANES, LANES), 0) + lax.broadcasted_iota(jnp.int32, (LANES, LANES), 1)
    flip = jnp.where(flip == LANES - 1, 1.0, 0.0)
    for t in range(LATS):
        south = jnp.broadcast_to(quad_v[pl.ds((5 - t) * LANES, LANES)].reshape(1, LANES), (8, LANES))
        south = jnp.dot(south, flip, preferred_element_type=f32, precision=lax.Precision.HIGHEST)
        lat_ref[t, 0:1, :] = lon_v[pl.ds(t * LANES, LANES)].reshape(1, LANES).astype(f32)
        lat_ref[t, 1:2, :] = quad_v[pl.ds(t * LANES, LANES)].reshape(1, LANES)
        lat_ref[t, 2:3, :] = south[0:1]

    for q in range(3):
        first = waves_ref[2 * q : 2 * q + 1, :]
        second = waves_ref[2 * q + 1 : 2 * q + 2, :]
        even_first = (first & 1) == 0
        even = jnp.where(even_first, first, second)
        odd = jnp.where(even_first, second, first)
        column[q] = jnp.broadcast_to(even.astype(f32), (LANES, LANES)).T
        column[3 + q] = jnp.broadcast_to(odd.astype(f32), (LANES, LANES)).T

    def table_block(step, carry):
        t = step // 6
        c = lax.rem(step, 6)
        parity = c // 3
        q = lax.rem(c, 3)
        points = lon_s[me + LANES * t]
        per_point = 1.0 / jnp.full((1, LANES), points, jnp.int32).astype(f32)
        wave = column[c]
        lane = lax.broadcasted_iota(jnp.int32, (1, LANES), 1).astype(f32)
        for block in range(WIDTH // LANES):
            turn = wave * (lane + float(block * LANES)) * per_point
            x = turn - jnp.floor(turn + 0.5)
            y = x * x
            rows = pl.ds(pl.multiple_of(q * LANES, LANES), LANES)
            columns = pl.ds(block * LANES, LANES)
            tables[t, 2 * parity, rows, columns] = horner(COSINE, y).astype(bf16)
            tables[t, 2 * parity + 1, rows, columns] = (horner(SINE, y) * x).astype(bf16)
        return carry

    lax.fori_loop(0, 2 * 6, table_block, 0)

    settle(send_one, recv_one, ssem_one, rsem_one)

    def widen(incoming):
        def body(i, carry):
            rows = pl.ds(pl.multiple_of(i * 128, 128), 128)
            wide[rows, :] = incoming[pl.ds(i * 16, 16)].astype(f32).reshape(128, LANES)
            return carry

        lax.fori_loop(0, 8, body, 0)
        for rv in range(8):
            planes[rv] = wide[pl.ds(rv, LANES, stride=8), :].T

    widen(recv_one)

    mass_sums[...] = jnp.zeros((SLOTS, 16, LANES), f32)
    for t in range(LATS):
        for j in range(SLOTS):
            base = (t * SLOTS + j) * 6 + 4
            for r in range(2):
                value = planes[r * 4, base : base + 2, :]
                for v in range(1, 4):
                    value = value + planes[r * 4 + v, base : base + 2, :]
                row = r * 6 + t * 2
                mass_sums[j, row : row + 2, :] = value
    mass_send[...] = mass_sums[...].astype(bf16)
    to_levels(mass_send, mass_recv, mass_ssem, mass_rsem)
    lax.fori_loop(2 * 6, LATS * 6, table_block, 0)

    for t in range(LATS):
        for r in range(2):
            for j in range(SLOTS):
                base = (t * SLOTS + j) * 6
                for v in range(4):
                    rv = r * 4 + v
                    pairs[t, r, j, v * 4 : v * 4 + 4, :] = planes[rv, base : base + 4, :]
                    pairs[t, r, j, 16 + v * 4 : 18 + v * 4, :] = planes[rv, base + 4 : base + 6, :]
    mass_lower[...] = from_levels(mass_send, mass_recv, mass_ssem, mass_rsem)
    for t in range(LATS):
        points = jnp.full((1, LANES), lon_s[me + LANES * t], jnp.int32)
        for r in range(2):
            for j in range(SLOTS):
                base = (t * SLOTS + j) * 6 + 4
                row = r * 6 + t * 2
                run = mass_lower[j, row : row + 2, :]
                for v in range(4):
                    run = run + planes[r * 4 + v, base : base + 2, :]
                    pairs[t, r, j, 18 + v * 4 : 20 + v * 4, :] = run * 0.25
        for q in range(3):
            first = waves_ref[2 * q : 2 * q + 1, :]
            second = waves_ref[2 * q + 1 : 2 * q + 2, :]
            even_first = (first & 1) == 0
            even = jnp.where(even_first, first, second)
            odd = jnp.where(even_first, second, first)
            sigma = 1.0 - (even & 2).astype(f32)
            tau = 1.0 - (odd & 2).astype(f32)
            even_factor = jnp.where(2 * even < points, jnp.where(even == 0, 1.0, 2.0), 0.0)
            odd_factor = jnp.where(2 * odd < points, 2.0, 0.0)
            pick = jnp.broadcast_to(even_first.astype(f32), (32, LANES)) > 0.5
            columns = slice(q * LANES, (q + 1) * LANES)
            real_even = jnp.where(pick, pairs[t, 0, 2 * q], pairs[t, 0, 2 * q + 1]) * even_factor
            real_odd = jnp.where(pick, pairs[t, 0, 2 * q + 1], pairs[t, 0, 2 * q]) * odd_factor
            imag_even = jnp.where(pick, pairs[t, 1, 2 * q], pairs[t, 1, 2 * q + 1]) * even_factor
            imag_odd = jnp.where(pick, pairs[t, 1, 2 * q + 1], pairs[t, 1, 2 * q]) * odd_factor
            left[t, 0, 0:32, columns] = real_even.astype(bf16)
            left[t, 0, 32:64, columns] = (sigma * real_even).astype(bf16)
            left[t, 1, 0:32, columns] = imag_even.astype(bf16)
            left[t, 1, 32:64, columns] = (sigma * imag_even).astype(bf16)
            left[t, 2, 0:32, columns] = real_odd.astype(bf16)
            left[t, 2, 32:64, columns] = (tau * imag_odd).astype(bf16)
            left[t, 3, 0:32, columns] = imag_odd.astype(bf16)
            left[t, 3, 32:64, columns] = (tau * real_odd).astype(bf16)

    def latitude(t, carry):
        whole_points = lon_s[me + LANES * t]
        for i in range(4):
            sumpq[i] = jnp.dot(left[t, i], tables[t, i], preferred_element_type=f32)
        lane = lax.broadcasted_iota(jnp.int32, (1, LANES), 1)
        for block in range(WIDTH // LANES):
            columns = slice(block * LANES, (block + 1) * LANES)
            k = lane + block * LANES
            points = jnp.full((1, LANES), whole_points, jnp.int32)
            share = jnp.where(8 * k < points, 1.0, jnp.where(8 * k == points, 0.5, 0.0))
            share = jnp.where(k == 0, 0.5, share)
            even_p, turn_p = sumpq[0, 0:32, columns], sumpq[0, 32:64, columns]
            even_m, turn_m = sumpq[1, 0:32, columns], sumpq[1, 32:64, columns]
            odd_p, side_m = sumpq[2, 0:32, columns], sumpq[2, 32:64, columns]
            odd_m, side_p = sumpq[3, 0:32, columns], sumpq[3, 32:64, columns]

            def product(grid):
                return grid[0:16] * grid[16:32] * share

            a, b = even_p - even_m, odd_p - odd_m
            f0p, f2p = product(a + b), product(a - b)
            a, b = even_p + even_m, odd_p + odd_m
            f0m, f2m = product(a + b), product(a - b)
            a, b = turn_p - turn_m, side_p + side_m
            f3p, f1p = product(a + b), product(a - b)
            a, b = turn_p + turn_m, side_p - side_m
            f1m, f3m = product(a + b), product(a - b)
            a, b = f0p + f2p, f0m + f2m
            leftback[0, 0:16, columns] = (a + b).astype(bf16)
            leftback[1, 0:16, columns] = (a - b).astype(bf16)
            a, b = f1p + f3p, f1m + f3m
            leftback[0, 16:32, columns] = (a + b).astype(bf16)
            leftback[1, 16:32, columns] = (a - b).astype(bf16)
            a, b = f0p - f2p, f0m - f2m
            leftback[2, 0:16, columns] = (a + b).astype(bf16)
            leftback[3, 0:16, columns] = (a - b).astype(bf16)
            a, b = f1p - f3p, f1m - f3m
            leftback[2, 16:32, columns] = (a + b).astype(bf16)
            leftback[3, 16:32, columns] = (b - a).astype(bf16)
        for i in range(4):
            sumpq[i, 0:32, 0:HALF] = lax.dot_general(
                leftback[i], tables[t, i], (((1,), (1,)), ((), ())), preferred_element_type=f32
            )
        north = quad_s[me + LANES * t]
        south = quad_s[2 * HALF - 1 - me - LANES * t]
        row = lax.broadcasted_iota(jnp.int32, (16, LANES), 0)
        points = jnp.full((1, LANES), whole_points, jnp.int32)
        weight = jnp.where((row & 1) == 0, north, south) * (ROOT / points.astype(f32))
        for q in range(3):
            first = waves_ref[2 * q : 2 * q + 1, :]
            second = waves_ref[2 * q + 1 : 2 * q + 2, :]
            even_first = (first & 1) == 0
            even = jnp.where(even_first, first, second)
            odd = jnp.where(even_first, second, first)
            sigma = 1.0 - (even & 2).astype(f32)
            tau = 1.0 - (odd & 2).astype(f32)
            even_weight = weight * (2 * even < points).astype(f32)
            odd_weight = weight * (2 * odd < points).astype(f32)
            pick = jnp.broadcast_to(even_first.astype(f32), (16, LANES)) > 0.5
            columns = slice(q * LANES, (q + 1) * LANES)
            real_even = (sumpq[0, 0:16, columns] + sigma * sumpq[0, 16:32, columns]) * even_weight
            imag_even = (sumpq[1, 0:16, columns] + sigma * sumpq[1, 16:32, columns]) * -even_weight
            real_odd = (sumpq[2, 0:16, columns] + tau * sumpq[3, 16:32, columns]) * odd_weight
            imag_odd = (sumpq[3, 0:16, columns] + tau * sumpq[2, 16:32, columns]) * -odd_weight
            for r, one, two in ((0, real_even, real_odd), (1, imag_even, imag_odd)):
                for j, value in ((2 * q, jnp.where(pick, one, two)), (2 * q + 1, jnp.where(pick, two, one))):
                    planes_two[t, r, j * 16 : j * 16 + 16, :] = value
        return carry

    lax.fori_loop(0, LATS, latitude, 0)

    for t in range(LATS):
        for r in range(2):
            wide[pl.ds(t * 256 + r, LANES, stride=2), :] = planes_two[t, r].T

    def narrow_two(i, carry):
        for t in range(LATS):
            value = wide[pl.ds(pl.multiple_of(t * 256 + i * 16, 16), 16), :]
            send_two[pl.ds(i * 8, 8), :, t * LANES : (t + 1) * LANES] = value.reshape(8, 2, LANES).astype(bf16)
        return carry

    lax.fori_loop(0, 16, narrow_two, 0)
    exchange(send_two, recv_two, ssem_two, rsem_two)
    def level_sum(value, first, second):
        row = lax.broadcasted_iota(jnp.int32, value.shape, 0)
        level = row & 3
        value = value + jnp.where(level >= 1, pltpu.roll(value, 1, 0), 0.0)
        value = value + jnp.where(level >= 2, pltpu.roll(value, 2, 0), 0.0)
        return (value + jnp.where(row < 4, first, second)) * 0.25

    def local(s, carry):
        m = slot_s[me * SLOTS + s]
        keep = (degree >= m).astype(f32)
        flipped = keep * (1.0 - 2.0 * ((degree + m) & 1).astype(f32))
        side = lax.broadcasted_iota(jnp.int32, (8, DEGREES), 0)
        extra = lower[s] * jnp.where(side < 4, keep, flipped)
        extra = jnp.concatenate([extra, jnp.zeros((8, DEGREES), f32)], axis=0).astype(bf16)
        product = jnp.dot(extra, legendre_ref[s], preferred_element_type=f32) * ROOT
        for t in range(LATS):
            low_four[t] = product[0:8, t * LANES : (t + 1) * LANES]
        row = lax.broadcasted_iota(jnp.int32, (8, LANES), 0)
        live = jnp.where((row < 4) | (m > 0), 1.0, 0.0)
        for t in range(LATS):
            inside = (2.0 * m.astype(f32) < lat_ref[t, 0:1, :]).astype(f32)
            for ns in range(2):
                factor = live * (inside * lat_ref[t, 1 + ns : 2 + ns, :])

                def rows(place, low):
                    return level_sum(
                        four[s, t, pl.ds(place + ns, 8, stride=8), :],
                        low_four[t, 4 * ns + low : 4 * ns + low + 1, :],
                        low_four[t, 4 * ns + low + 2 : 4 * ns + low + 3, :],
                    )

                weighted[s, t, ns * 16 + 8 : ns * 16 + 16, :] = rows(2, 1) * factor
                weighted[s, t, 32 + ns * 16 + 8 : 32 + ns * 16 + 16, :] = (
                    four[s, t, pl.ds(6 + ns, 8, stride=8), :] + rows(4, 0)
                ) * factor
        return carry

    total = from_levels(lev_send, lev_recv, lev_ssem, lev_rsem)
    sums[...] = total
    for s in range(SLOTS):
        lower[s, 0:4, :] = sums[s * 4 : s * 4 + 4, :]
        lower[s, 4:8, :] = sums[s * 4 : s * 4 + 4, :]
    lax.fori_loop(0, SLOTS, local, 0)

    settle(send_two, recv_two, ssem_two, rsem_two)

    def widen_two(i, carry):
        for t in range(LATS):
            value = recv_two[pl.ds(i * 8, 8), :, t * LANES : (t + 1) * LANES].astype(f32)
            wide[pl.ds(pl.multiple_of(t * 256 + i * 16, 16), 16), :] = value.reshape(16, LANES)
        return carry

    lax.fori_loop(0, 16, widen_two, 0)
    for t in range(LATS):
        for r in range(2):
            planes[r] = wide[pl.ds(t * 256 + r, LANES, stride=2), :].T
            for j in range(SLOTS):
                for v in range(4):
                    row = j * 16 + v * 4
                    weighted[j, t, pl.ds(r * 4 + v, 4, stride=16), :] = planes[r, row : row + 4, :]

    def direct(s, carry):
        m = slot_s[me * SLOTS + s]
        keep = (degree >= m).astype(f32) * ROOT
        flipped = keep * (1.0 - 2.0 * ((degree + m) & 1).astype(f32))
        operand = jnp.concatenate([weighted[s, t] for t in range(LATS)], axis=1).astype(bf16)
        product = lax.dot_general(
            operand, legendre_ref[s], (((1,), (1,)), ((), ())), preferred_element_type=f32
        )
        for x in range(2):
            for y in range(2):
                row = x * 32 + y * 8
                value = product[row : row + 8] * keep + product[row + 16 : row + 24] * flipped
                out_ref[s, 0, 2 * x + y] = value[0:4].astype(bf16)
                out_ref[s, 1, 2 * x + y] = value[4:8].astype(bf16)
        return carry

    lax.fori_loop(0, SLOTS, direct, 0)


def per_device(coeffs, legendre, slot_wave, lon_points, quad_weights):
    vmem = pl.BlockSpec(memory_space=pltpu.VMEM)
    outside = pl.BlockSpec(memory_space=pltpu.HBM)
    scratch = [
        pltpu.SMEM((DEGREES,), jnp.int32),
        pltpu.SMEM((DEGREES,), jnp.int32),
        pltpu.SMEM((DEGREES,), f32),
        pltpu.VMEM((DEGREES,), jnp.int32),
        pltpu.VMEM((DEGREES,), jnp.int32),
        pltpu.VMEM((DEGREES,), f32),
        pltpu.VMEM(coeffs.shape, bf16),
        pltpu.VMEM(legendre.shape, bf16),
        pltpu.VMEM((8, LANES), jnp.int32),
        pltpu.VMEM((LATS, 8, LANES), f32),
        pltpu.VMEM((32, DEGREES), f32),
        pltpu.VMEM((32, DEGREES), bf16),
        pltpu.VMEM((LEV, 32, DEGREES), bf16),
        pltpu.VMEM((SLOTS, 8, DEGREES), f32),
        pltpu.VMEM((DEGREES // LANES, 64, LANES), f32),
        pltpu.VMEM((SLOTS, LATS, 64, LANES), f32),
        pltpu.VMEM((6, LANES, LANES), f32),
        pltpu.VMEM((LATS, 4, HALF, WIDTH), bf16),
        pltpu.VMEM((8, LANES, LANES), f32),
        pltpu.VMEM((8 * LANES, LANES), f32),
        pltpu.VMEM((WAVE, 8, LANES), bf16),
        pltpu.VMEM((WAVE, 8, LANES), bf16),
        pltpu.VMEM((WAVE, 2, HALF), bf16),
        pltpu.VMEM((WAVE, 2, HALF), bf16),
        pltpu.VMEM((LATS, 2, SLOTS, 32, LANES), f32),
        pltpu.VMEM((LATS, 4, 64, HALF), bf16),
        pltpu.VMEM((4, 64, WIDTH), f32),
        pltpu.VMEM((4, 32, WIDTH), bf16),
        pltpu.VMEM((LATS, 2, LANES, LANES), f32),
        pltpu.VMEM((SLOTS, LATS, 64, LANES), f32),
        pltpu.VMEM((SLOTS, 16, LANES), f32),
        pltpu.VMEM((SLOTS, 16, LANES), bf16),
        pltpu.VMEM((LEV, SLOTS, 16, LANES), bf16),
        pltpu.VMEM((SLOTS, 16, LANES), f32),
        pltpu.VMEM((LATS, 8, LANES), f32),
        pltpu.SemaphoreType.DMA((6,)),
        pltpu.SemaphoreType.DMA(()),
        pltpu.SemaphoreType.DMA((SLOTS,)),
    ] + [pltpu.SemaphoreType.DMA(())] * 8
    return pl.pallas_call(
        kernel,
        out_shape=jax.ShapeDtypeStruct(coeffs.shape, bf16),
        in_specs=[outside] * 5,
        out_specs=vmem,
        scratch_shapes=scratch,
        compiler_params=pltpu.CompilerParams(
            collective_id=0, has_side_effects=True, vmem_limit_bytes=63 * 1024 * 1024
        ),
    )(lon_points, slot_wave, quad_weights, coeffs, legendre)


def solution(mesh):
    placed = (P("wave", None, None, "lev", None), P("wave", None, None), P(), P(), P())
    return jax.shard_map(
        per_device,
        mesh=mesh,
        in_specs=placed,
        out_specs=P("wave", None, None, "lev", None),
        check_vma=False,
    )
```

```python
import math

import numpy as np
import jax
import jax.numpy as jnp
from jax import lax
from jax.experimental import pallas as pl
from jax.experimental.pallas import tpu as pltpu
from jax.sharding import PartitionSpec as P

MESH = pl.DeviceIdType.MESH
f32 = jnp.float32
bf16 = jnp.bfloat16
SLOTS = 6
DEGREES = 768
HALF = 384
WAVE = 128
LEV = 4
LATS = 3
LANES = 128
WIDTH = 512
ROOT = 1.0 / math.sqrt(768.0)


def turn_polynomials(terms):
    x = np.cos(np.linspace(0.0, np.pi, 4001)) * 0.5
    y = x * x
    powers = np.stack([y**i for i in range(terms)], axis=1)
    cosine = np.linalg.lstsq(powers, np.cos(2 * np.pi * x), rcond=None)[0]
    sine = np.linalg.lstsq(powers * x[:, None], np.sin(2 * np.pi * x), rcond=None)[0]
    return [float(np.float32(c)) for c in cosine], [float(np.float32(c)) for c in sine]


COSINE, SINE = turn_polynomials(6)


def horner(coefficients, y):
    total = coefficients[-1]
    for c in coefficients[-2::-1]:
        total = total * y + c
    return total


def kernel(
    lon_h, slot_h, quad_h, coeffs_h, legendre_h, out_ref,
    lon_s, slot_s, quad_s, lon_v, slot_v, quad_v, coeffs_ref, legendre_ref, waves_ref, lat_ref,
    sums, lev_send, lev_recv, lower, stage, four, column, tables, planes, wide,
    send_one, recv_one, send_two, recv_two, pairs, left, sumpq, leftback, planes_two, weighted,
    mass_sums, mass_send, mass_recv, mass_lower, low_four,
    result, small_sem, coeffs_sem, legendre_sem, store_sem,
    lev_ssem, lev_rsem, mass_ssem, mass_rsem, ssem_one, rsem_one, ssem_two, rsem_two,
):
    me = lax.axis_index("wave")
    lev = lax.axis_index("lev")
    barrier = pltpu.get_barrier_semaphore()
    small = [
        pltpu.make_async_copy(src, dst, small_sem.at[i])
        for i, (src, dst) in enumerate(
            ((slot_h, slot_s), (lon_h, lon_s), (quad_h, quad_s), (slot_h, slot_v), (lon_h, lon_v), (quad_h, quad_v))
        )
    ]
    load_coeffs = pltpu.make_async_copy(coeffs_h, coeffs_ref, coeffs_sem)

    def load_legendre(s):
        return pltpu.make_async_copy(legendre_h.at[s], legendre_ref.at[s], legendre_sem.at[s])

    small[0].start()
    load_coeffs.start()
    for s in range(SLOTS):
        load_legendre(s).start()
    for copy in small[1:]:
        copy.start()
    for i in range(1, LEV):
        pl.semaphore_signal(barrier, inc=1, device_id=(me, lax.rem(lev + i, LEV)), device_id_type=MESH)

    def greet(i, carry):
        pl.semaphore_signal(barrier, inc=1, device_id=(lax.rem(me + i, WAVE), lev), device_id_type=MESH)
        return carry

    lax.fori_loop(1, WAVE, greet, 0)
    small[0].wait()
    load_coeffs.wait()

    degree = lax.broadcasted_iota(jnp.int32, (1, DEGREES), 1)
    place = (0, 4, 2, 6)

    def put_rows(start, stride, value):
        for b in range(DEGREES // LANES):
            stage[b, pl.ds(start, 4, stride=stride), :] = value[:, b * LANES : (b + 1) * LANES]

    def forward(s, carry):
        load_legendre(s).wait()
        m = slot_s[me * SLOTS + s]
        keep = (degree >= m).astype(f32)
        flipped = keep * (1.0 - 2.0 * ((degree + m) & 1).astype(f32))
        for r in range(2):
            for f in range(4):
                value = coeffs_ref[s, r, f].astype(f32)
                put_rows(r * 32 + place[f], 8, value * keep)
                put_rows(r * 32 + place[f] + 1, 8, value * flipped)
        operand = jnp.concatenate([stage[b] for b in range(DEGREES // LANES)], axis=1).astype(bf16)
        product = jnp.dot(operand, legendre_ref[s], preferred_element_type=f32) * ROOT
        for t in range(LATS):
            four[s, t] = product[:, t * LANES : (t + 1) * LANES]
        return carry

    lax.fori_loop(0, SLOTS, forward, 0)

    sums[24:32, :] = jnp.zeros((8, DEGREES), f32)
    for s in range(SLOTS):
        for r in range(2):
            for f in (1, 2):
                row = s * 4 + r * 2 + f - 1
                sums[row : row + 1, :] = jnp.sum(coeffs_ref[s, r, f].astype(f32), axis=0, keepdims=True)
    lev_send[...] = sums[...].astype(bf16)

    def to_levels(outgoing, incoming, ssem, rsem):
        for i in range(1, LEV):
            pltpu.make_async_remote_copy(
                src_ref=outgoing, dst_ref=incoming.at[lev], send_sem=ssem, recv_sem=rsem,
                device_id=(me, lax.rem(lev + i, LEV)), device_id_type=MESH,
            ).start()

    def from_levels(outgoing, incoming, ssem, rsem):
        part = incoming.at[pl.ds(0, LEV - 1)]
        pltpu.make_async_copy(part, part, rsem).wait()
        pltpu.make_async_copy(part, part, ssem).wait()
        total = jnp.zeros(outgoing.shape, f32)
        for k in range(LEV):
            total = total + jnp.where(k < lev, incoming[k].astype(f32), 0.0)
        return total

    def spread(step, carry):
        planes[step, 104:128, :] = jnp.zeros((24, LANES), f32)
        for t in range(LATS):
            for j in range(SLOTS):
                base = (t * SLOTS + j) * 6
                planes[step, base : base + 6, :] = four[j, t, pl.ds(pl.multiple_of(step * 8, 8), 8), :][0:6]
        return carry

    lax.fori_loop(0, 8, spread, 0)
    for rv in range(8):
        wide[pl.ds(rv, LANES, stride=8), :] = planes[rv].T

    def narrow_one(i, carry):
        rows = pl.ds(pl.multiple_of(i * 128, 128), 128)
        send_one[pl.ds(i * 16, 16)] = wide[rows, :].reshape(16, 8, LANES).astype(bf16)
        return carry

    lax.fori_loop(0, 8, narrow_one, 0)

    def exchange(outgoing, incoming, ssem, rsem):
        pltpu.make_async_copy(outgoing.at[me], incoming.at[me], rsem).start()

        def put(peer):
            pltpu.make_async_remote_copy(
                src_ref=outgoing.at[peer], dst_ref=incoming.at[me], send_sem=ssem, recv_sem=rsem,
                device_id=(peer, lev), device_id_type=MESH,
            ).start()

        put(lax.rem(me + WAVE // 2, WAVE))

        def both(i, carry):
            put(lax.rem(me + WAVE // 2 - i, WAVE))
            put(lax.rem(me + WAVE // 2 + i, WAVE))
            return carry

        lax.fori_loop(1, WAVE // 2, both, 0)

    def settle(outgoing, incoming, ssem, rsem):
        pltpu.make_async_copy(incoming, incoming, rsem).wait()
        part = outgoing.at[pl.ds(0, WAVE - 1)]
        pltpu.make_async_copy(part, part, ssem).wait()

    lev_recv[lev] = jnp.zeros((32, DEGREES), bf16)
    mass_recv[lev] = jnp.zeros((SLOTS, 16, LANES), bf16)
    pl.semaphore_wait(barrier, WAVE - 1 + LEV - 1)
    exchange(send_one, recv_one, ssem_one, rsem_one)
    to_levels(lev_send, lev_recv, lev_ssem, lev_rsem)
    for copy in small[1:]:
        copy.wait()

    planes_two[:, :, 96:LANES, :] = jnp.zeros((LATS, 2, LANES - 96, LANES), f32)

    number = lax.broadcasted_iota(jnp.int32, (8, DEGREES), 1).astype(f32)
    group = jnp.floor((number + 0.5) * (1.0 / SLOTS))
    mine = (number - group * SLOTS) == lax.broadcasted_iota(jnp.int32, (8, DEGREES), 0).astype(f32)
    every = jnp.concatenate([slot_v[pl.ds(b * LANES, LANES)].reshape(1, LANES) for b in range(6)], axis=1)
    high = jnp.where(mine, (every >> 4).astype(f32), 0.0)
    low = jnp.where(mine, (every & 15).astype(f32), 0.0)
    ahead = lax.broadcasted_iota(jnp.int32, (DEGREES, LANES), 0) - SLOTS * lax.broadcasted_iota(
        jnp.int32, (DEGREES, LANES), 1
    )
    belongs = jnp.where((ahead >= 0) & (ahead < SLOTS), 1.0, 0.0).astype(bf16)
    split = jnp.dot(
        jnp.concatenate([high, low], axis=0).astype(bf16), belongs, preferred_element_type=f32
    )
    waves_ref[...] = (split[0:8] * 16.0 + split[8:16]).astype(jnp.int32)
    flip = lax.broadcasted_iota(jnp.int32, (LANES, LANES), 0) + lax.broadcasted_iota(jnp.int32, (LANES, LANES), 1)
    flip = jnp.where(flip == LANES - 1, 1.0, 0.0)
    for t in range(LATS):
        south = jnp.broadcast_to(quad_v[pl.ds((5 - t) * LANES, LANES)].reshape(1, LANES), (8, LANES))
        south = jnp.dot(south, flip, preferred_element_type=f32, precision=lax.Precision.HIGHEST)
        lat_ref[t, 0:1, :] = lon_v[pl.ds(t * LANES, LANES)].reshape(1, LANES).astype(f32)
        lat_ref[t, 1:2, :] = quad_v[pl.ds(t * LANES, LANES)].reshape(1, LANES)
        lat_ref[t, 2:3, :] = south[0:1]

    for q in range(3):
        first = waves_ref[2 * q : 2 * q + 1, :]
        second = waves_ref[2 * q + 1 : 2 * q + 2, :]
        even_first = (first & 1) == 0
        even = jnp.where(even_first, first, second)
        odd = jnp.where(even_first, second, first)
        column[q] = jnp.broadcast_to(even.astype(f32), (LANES, LANES)).T
        column[3 + q] = jnp.broadcast_to(odd.astype(f32), (LANES, LANES)).T

    def table_block(step, carry):
        t = step // 6
        c = lax.rem(step, 6)
        parity = c // 3
        q = lax.rem(c, 3)
        points = lon_s[me + LANES * t]
        per_point = 1.0 / jnp.full((1, LANES), points, jnp.int32).astype(f32)
        wave = column[c]
        lane = lax.broadcasted_iota(jnp.int32, (1, LANES), 1).astype(f32)
        for block in range(WIDTH // LANES):
            turn = wave * (lane + float(block * LANES)) * per_point
            x = turn - jnp.floor(turn + 0.5)
            y = x * x
            rows = pl.ds(pl.multiple_of(q * LANES, LANES), LANES)
            columns = pl.ds(block * LANES, LANES)
            tables[t, 2 * parity, rows, columns] = horner(COSINE, y).astype(bf16)
            tables[t, 2 * parity + 1, rows, columns] = (horner(SINE, y) * x).astype(bf16)
        return carry

    lax.fori_loop(0, 2 * 6, table_block, 0)

    settle(send_one, recv_one, ssem_one, rsem_one)

    def widen(incoming):
        def body(i, carry):
            rows = pl.ds(pl.multiple_of(i * 128, 128), 128)
            wide[rows, :] = incoming[pl.ds(i * 16, 16)].astype(f32).reshape(128, LANES)
            return carry

        lax.fori_loop(0, 8, body, 0)
        for rv in range(8):
            planes[rv] = wide[pl.ds(rv, LANES, stride=8), :].T

    widen(recv_one)

    mass_sums[...] = jnp.zeros((SLOTS, 16, LANES), f32)
    for t in range(LATS):
        for j in range(SLOTS):
            base = (t * SLOTS + j) * 6 + 4
            for r in range(2):
                value = planes[r * 4, base : base + 2, :]
                for v in range(1, 4):
                    value = value + planes[r * 4 + v, base : base + 2, :]
                row = r * 6 + t * 2
                mass_sums[j, row : row + 2, :] = value
    mass_send[...] = mass_sums[...].astype(bf16)
    to_levels(mass_send, mass_recv, mass_ssem, mass_rsem)
    lax.fori_loop(2 * 6, LATS * 6, table_block, 0)

    for t in range(LATS):
        for r in range(2):
            for j in range(SLOTS):
                base = (t * SLOTS + j) * 6
                for v in range(4):
                    rv = r * 4 + v
                    pairs[t, r, j, v * 4 : v * 4 + 4, :] = planes[rv, base : base + 4, :]
                    pairs[t, r, j, 16 + v * 4 : 18 + v * 4, :] = planes[rv, base + 4 : base + 6, :]
    mass_lower[...] = from_levels(mass_send, mass_recv, mass_ssem, mass_rsem)
    for t in range(LATS):
        points = jnp.full((1, LANES), lon_s[me + LANES * t], jnp.int32)
        for r in range(2):
            for j in range(SLOTS):
                base = (t * SLOTS + j) * 6 + 4
                row = r * 6 + t * 2
                run = mass_lower[j, row : row + 2, :]
                for v in range(4):
                    run = run + planes[r * 4 + v, base : base + 2, :]
                    pairs[t, r, j, 18 + v * 4 : 20 + v * 4, :] = run * 0.25
        for q in range(3):
            first = waves_ref[2 * q : 2 * q + 1, :]
            second = waves_ref[2 * q + 1 : 2 * q + 2, :]
            even_first = (first & 1) == 0
            even = jnp.where(even_first, first, second)
            odd = jnp.where(even_first, second, first)
            sigma = 1.0 - (even & 2).astype(f32)
            tau = 1.0 - (odd & 2).astype(f32)
            even_factor = jnp.where(2 * even < points, jnp.where(even == 0, 1.0, 2.0), 0.0)
            odd_factor = jnp.where(2 * odd < points, 2.0, 0.0)
            pick = jnp.broadcast_to(even_first.astype(f32), (32, LANES)) > 0.5
            columns = slice(q * LANES, (q + 1) * LANES)
            real_even = jnp.where(pick, pairs[t, 0, 2 * q], pairs[t, 0, 2 * q + 1]) * even_factor
            real_odd = jnp.where(pick, pairs[t, 0, 2 * q + 1], pairs[t, 0, 2 * q]) * odd_factor
            imag_even = jnp.where(pick, pairs[t, 1, 2 * q], pairs[t, 1, 2 * q + 1]) * even_factor
            imag_odd = jnp.where(pick, pairs[t, 1, 2 * q + 1], pairs[t, 1, 2 * q]) * odd_factor
            left[t, 0, 0:32, columns] = real_even.astype(bf16)
            left[t, 0, 32:64, columns] = (sigma * real_even).astype(bf16)
            left[t, 1, 0:32, columns] = imag_even.astype(bf16)
            left[t, 1, 32:64, columns] = (sigma * imag_even).astype(bf16)
            left[t, 2, 0:32, columns] = real_odd.astype(bf16)
            left[t, 2, 32:64, columns] = (tau * imag_odd).astype(bf16)
            left[t, 3, 0:32, columns] = imag_odd.astype(bf16)
            left[t, 3, 32:64, columns] = (tau * real_odd).astype(bf16)

    def latitude(t, carry):
        whole_points = lon_s[me + LANES * t]
        for i in range(4):
            sumpq[i] = jnp.dot(left[t, i], tables[t, i], preferred_element_type=f32)
        lane = lax.broadcasted_iota(jnp.int32, (1, LANES), 1)
        for block in range(WIDTH // LANES):
            columns = slice(block * LANES, (block + 1) * LANES)
            k = lane + block * LANES
            points = jnp.full((1, LANES), whole_points, jnp.int32)
            share = jnp.where(8 * k < points, 1.0, jnp.where(8 * k == points, 0.5, 0.0))
            share = jnp.where(k == 0, 0.5, share)
            even_p, turn_p = sumpq[0, 0:32, columns], sumpq[0, 32:64, columns]
            even_m, turn_m = sumpq[1, 0:32, columns], sumpq[1, 32:64, columns]
            odd_p, side_m = sumpq[2, 0:32, columns], sumpq[2, 32:64, columns]
            odd_m, side_p = sumpq[3, 0:32, columns], sumpq[3, 32:64, columns]

            def product(grid):
                return grid[0:16] * grid[16:32] * share

            a, b = even_p - even_m, odd_p - odd_m
            f0p, f2p = product(a + b), product(a - b)
            a, b = even_p + even_m, odd_p + odd_m
            f0m, f2m = product(a + b), product(a - b)
            a, b = turn_p - turn_m, side_p + side_m
            f3p, f1p = product(a + b), product(a - b)
            a, b = turn_p + turn_m, side_p - side_m
            f1m, f3m = product(a + b), product(a - b)
            a, b = f0p + f2p, f0m + f2m
            leftback[0, 0:16, columns] = (a + b).astype(bf16)
            leftback[1, 0:16, columns] = (a - b).astype(bf16)
            a, b = f1p + f3p, f1m + f3m
            leftback[0, 16:32, columns] = (a + b).astype(bf16)
            leftback[1, 16:32, columns] = (a - b).astype(bf16)
            a, b = f0p - f2p, f0m - f2m
            leftback[2, 0:16, columns] = (a + b).astype(bf16)
            leftback[3, 0:16, columns] = (a - b).astype(bf16)
            a, b = f1p - f3p, f1m - f3m
            leftback[2, 16:32, columns] = (a + b).astype(bf16)
            leftback[3, 16:32, columns] = (b - a).astype(bf16)
        for i in range(4):
            sumpq[i, 0:32, 0:HALF] = lax.dot_general(
                leftback[i], tables[t, i], (((1,), (1,)), ((), ())), preferred_element_type=f32
            )
        north = quad_s[me + LANES * t]
        south = quad_s[2 * HALF - 1 - me - LANES * t]
        row = lax.broadcasted_iota(jnp.int32, (16, LANES), 0)
        points = jnp.full((1, LANES), whole_points, jnp.int32)
        weight = jnp.where((row & 1) == 0, north, south) * (ROOT / points.astype(f32))
        for q in range(3):
            first = waves_ref[2 * q : 2 * q + 1, :]
            second = waves_ref[2 * q + 1 : 2 * q + 2, :]
            even_first = (first & 1) == 0
            even = jnp.where(even_first, first, second)
            odd = jnp.where(even_first, second, first)
            sigma = 1.0 - (even & 2).astype(f32)
            tau = 1.0 - (odd & 2).astype(f32)
            even_weight = weight * (2 * even < points).astype(f32)
            odd_weight = weight * (2 * odd < points).astype(f32)
            pick = jnp.broadcast_to(even_first.astype(f32), (16, LANES)) > 0.5
            columns = slice(q * LANES, (q + 1) * LANES)
            real_even = (sumpq[0, 0:16, columns] + sigma * sumpq[0, 16:32, columns]) * even_weight
            imag_even = (sumpq[1, 0:16, columns] + sigma * sumpq[1, 16:32, columns]) * -even_weight
            real_odd = (sumpq[2, 0:16, columns] + tau * sumpq[3, 16:32, columns]) * odd_weight
            imag_odd = (sumpq[3, 0:16, columns] + tau * sumpq[2, 16:32, columns]) * -odd_weight
            for r, one, two in ((0, real_even, real_odd), (1, imag_even, imag_odd)):
                for j, value in ((2 * q, jnp.where(pick, one, two)), (2 * q + 1, jnp.where(pick, two, one))):
                    planes_two[t, r, j * 16 : j * 16 + 16, :] = value
        return carry

    lax.fori_loop(0, LATS, latitude, 0)

    for t in range(LATS):
        for r in range(2):
            wide[pl.ds(t * 256 + r, LANES, stride=2), :] = planes_two[t, r].T

    def narrow_two(i, carry):
        for t in range(LATS):
            value = wide[pl.ds(pl.multiple_of(t * 256 + i * 16, 16), 16), :]
            send_two[pl.ds(i * 8, 8), :, t * LANES : (t + 1) * LANES] = value.reshape(8, 2, LANES).astype(bf16)
        return carry

    lax.fori_loop(0, 16, narrow_two, 0)
    exchange(send_two, recv_two, ssem_two, rsem_two)
    def level_sum(value, first, second):
        row = lax.broadcasted_iota(jnp.int32, value.shape, 0)
        level = row & 3
        value = value + jnp.where(level >= 1, pltpu.roll(value, 1, 0), 0.0)
        value = value + jnp.where(level >= 2, pltpu.roll(value, 2, 0), 0.0)
        return (value + jnp.where(row < 4, first, second)) * 0.25

    def local(s, carry):
        m = slot_s[me * SLOTS + s]
        keep = (degree >= m).astype(f32)
        flipped = keep * (1.0 - 2.0 * ((degree + m) & 1).astype(f32))
        side = lax.broadcasted_iota(jnp.int32, (8, DEGREES), 0)
        extra = lower[s] * jnp.where(side < 4, keep, flipped)
        extra = jnp.concatenate([extra, jnp.zeros((8, DEGREES), f32)], axis=0).astype(bf16)
        product = jnp.dot(extra, legendre_ref[s], preferred_element_type=f32) * ROOT
        for t in range(LATS):
            low_four[t] = product[0:8, t * LANES : (t + 1) * LANES]
        row = lax.broadcasted_iota(jnp.int32, (8, LANES), 0)
        live = jnp.where((row < 4) | (m > 0), 1.0, 0.0)
        for t in range(LATS):
            inside = (2.0 * m.astype(f32) < lat_ref[t, 0:1, :]).astype(f32)
            for ns in range(2):
                factor = live * (inside * lat_ref[t, 1 + ns : 2 + ns, :])

                def rows(place, low):
                    return level_sum(
                        four[s, t, pl.ds(place + ns, 8, stride=8), :],
                        low_four[t, 4 * ns + low : 4 * ns + low + 1, :],
                        low_four[t, 4 * ns + low + 2 : 4 * ns + low + 3, :],
                    )

                weighted[s, t, ns * 16 + 8 : ns * 16 + 16, :] = rows(2, 1) * factor
                weighted[s, t, 32 + ns * 16 + 8 : 32 + ns * 16 + 16, :] = (
                    four[s, t, pl.ds(6 + ns, 8, stride=8), :] + rows(4, 0)
                ) * factor
        return carry

    total = from_levels(lev_send, lev_recv, lev_ssem, lev_rsem)
    sums[...] = total
    for s in range(SLOTS):
        lower[s, 0:4, :] = sums[s * 4 : s * 4 + 4, :]
        lower[s, 4:8, :] = sums[s * 4 : s * 4 + 4, :]
    lax.fori_loop(0, SLOTS, local, 0)

    settle(send_two, recv_two, ssem_two, rsem_two)

    def widen_two(i, carry):
        for t in range(LATS):
            value = recv_two[pl.ds(i * 8, 8), :, t * LANES : (t + 1) * LANES].astype(f32)
            wide[pl.ds(pl.multiple_of(t * 256 + i * 16, 16), 16), :] = value.reshape(16, LANES)
        return carry

    lax.fori_loop(0, 16, widen_two, 0)
    for t in range(LATS):
        for r in range(2):
            planes[r] = wide[pl.ds(t * 256 + r, LANES, stride=2), :].T
            for j in range(SLOTS):
                for v in range(4):
                    row = j * 16 + v * 4
                    weighted[j, t, pl.ds(r * 4 + v, 4, stride=16), :] = planes[r, row : row + 4, :]

    def store(s):
        return pltpu.make_async_copy(result.at[s], out_ref.at[s], store_sem.at[s])

    def direct(s, carry):
        m = slot_s[me * SLOTS + s]
        keep = (degree >= m).astype(f32) * ROOT
        flipped = keep * (1.0 - 2.0 * ((degree + m) & 1).astype(f32))
        operand = jnp.concatenate([weighted[s, t] for t in range(LATS)], axis=1).astype(bf16)
        product = lax.dot_general(
            operand, legendre_ref[s], (((1,), (1,)), ((), ())), preferred_element_type=f32
        )
        for x in range(2):
            for y in range(2):
                row = x * 32 + y * 8
                value = product[row : row + 8] * keep + product[row + 16 : row + 24] * flipped
                result[s, 0, 2 * x + y] = value[0:4].astype(bf16)
                result[s, 1, 2 * x + y] = value[4:8].astype(bf16)
        store(s).start()
        return carry

    lax.fori_loop(0, SLOTS, direct, 0)
    for s in range(SLOTS):
        store(s).wait()


def per_device(coeffs, legendre, slot_wave, lon_points, quad_weights):
    outside = pl.BlockSpec(memory_space=pltpu.HBM)
    scratch = [
        pltpu.SMEM((DEGREES,), jnp.int32),
        pltpu.SMEM((DEGREES,), jnp.int32),
        pltpu.SMEM((DEGREES,), f32),
        pltpu.VMEM((DEGREES,), jnp.int32),
        pltpu.VMEM((DEGREES,), jnp.int32),
        pltpu.VMEM((DEGREES,), f32),
        pltpu.VMEM(coeffs.shape, bf16),
        pltpu.VMEM(legendre.shape, bf16),
        pltpu.VMEM((8, LANES), jnp.int32),
        pltpu.VMEM((LATS, 8, LANES), f32),
        pltpu.VMEM((32, DEGREES), f32),
        pltpu.VMEM((32, DEGREES), bf16),
        pltpu.VMEM((LEV, 32, DEGREES), bf16),
        pltpu.VMEM((SLOTS, 8, DEGREES), f32),
        pltpu.VMEM((DEGREES // LANES, 64, LANES), f32),
        pltpu.VMEM((SLOTS, LATS, 64, LANES), f32),
        pltpu.VMEM((6, LANES, LANES), f32),
        pltpu.VMEM((LATS, 4, HALF, WIDTH), bf16),
        pltpu.VMEM((8, LANES, LANES), f32),
        pltpu.VMEM((8 * LANES, LANES), f32),
        pltpu.VMEM((WAVE, 8, LANES), bf16),
        pltpu.VMEM((WAVE, 8, LANES), bf16),
        pltpu.VMEM((WAVE, 2, HALF), bf16),
        pltpu.VMEM((WAVE, 2, HALF), bf16),
        pltpu.VMEM((LATS, 2, SLOTS, 32, LANES), f32),
        pltpu.VMEM((LATS, 4, 64, HALF), bf16),
        pltpu.VMEM((4, 64, WIDTH), f32),
        pltpu.VMEM((4, 32, WIDTH), bf16),
        pltpu.VMEM((LATS, 2, LANES, LANES), f32),
        pltpu.VMEM((SLOTS, LATS, 64, LANES), f32),
        pltpu.VMEM((SLOTS, 16, LANES), f32),
        pltpu.VMEM((SLOTS, 16, LANES), bf16),
        pltpu.VMEM((LEV, SLOTS, 16, LANES), bf16),
        pltpu.VMEM((SLOTS, 16, LANES), f32),
        pltpu.VMEM((LATS, 8, LANES), f32),
        pltpu.VMEM(coeffs.shape, bf16),
        pltpu.SemaphoreType.DMA((6,)),
        pltpu.SemaphoreType.DMA(()),
        pltpu.SemaphoreType.DMA((SLOTS,)),
        pltpu.SemaphoreType.DMA((SLOTS,)),
    ] + [pltpu.SemaphoreType.DMA(())] * 8
    return pl.pallas_call(
        kernel,
        out_shape=jax.ShapeDtypeStruct(coeffs.shape, bf16),
        in_specs=[outside] * 5,
        out_specs=outside,
        scratch_shapes=scratch,
        compiler_params=pltpu.CompilerParams(
            collective_id=0, has_side_effects=True, vmem_limit_bytes=63 * 1024 * 1024
        ),
    )(lon_points, slot_wave, quad_weights, coeffs, legendre)


def solution(mesh):
    placed = (P("wave", None, None, "lev", None), P("wave", None, None), P(), P(), P())
    return jax.shard_map(
        per_device,
        mesh=mesh,
        in_specs=placed,
        out_specs=P("wave", None, None, "lev", None),
        check_vma=False,
    )
```
